32 devices in a mesh: rep: 16 (over z, y, x), shard: 2 (over core).
Axes of the slice: x: 2, y: 2, z: 4, core: 2. Of those that a mesh axis runs over, the one named last changes fastest.
Arguments:
- tokens: bfloat16 [8192, 1024], P(('rep', 'shard')), may hold values from -6 to 6
- lengths: int32 [32, 4], P(('rep', 'shard')), may hold values from 1 to 253, as said below
- norm_gain: bfloat16 [1024], P('shard'), may hold values from 0.099609375 to 1.8984375
- in_weight: bfloat16 [1024, 4384], P('shard'), may hold values from -0.1875 to 0.1875
- conv_weight: bfloat16 [2304, 4], P('shard'), may hold values from -3 to 3
- conv_bias: bfloat16 [2304], P('shard'), may hold values from -3 to 3
- step_bias: bfloat16 [32], P('shard'), may hold values from -7 to -2.5
- decay_log: bfloat16 [32], P('shard'), may hold values from 0 to 2.796875
- skip_gain: bfloat16 [32], P('shard'), may hold values from 0.5 to 2
- gate_gain: bfloat16 [2048], P('shard'), may hold values from 0.099609375 to 1.8984375
- out_weight: bfloat16 [2048, 1024], P('shard'), may hold values from -0.125 to 0.125
- cotangent: bfloat16 [8192, 1024], P(('rep', 'shard')), may hold values from -6 to 6
Outputs:
- output: bfloat16 [8192, 1024], P(('rep', 'shard'))
- input_grad: float32 [8192, 1024], P(('rep', 'shard'))
- norm_gain_grad: float32 [1024], P('shard')
- in_weight_grad: float32 [1024, 4384], P('shard')
- conv_weight_grad: float32 [2304, 4], P('shard')
- conv_bias_grad: float32 [2304], P('shard')
- step_bias_grad: float32 [32], P('shard')
- decay_log_grad: float32 [32], P('shard')
- skip_gain_grad: float32 [32], P('shard')
- gate_gain_grad: float32 [2048], P('shard')
- out_weight_grad: float32 [2048, 1024], P('shard')
The draws below stay inside these ranges and needn't reach their ends.
Inputs may be any that keep to these rules, and one draw needn't show every extreme that they name: `lengths`: each device's sequences fill its first rows in order and hold 256 rows at most, exactly so on some device; the rows after them are padding.
All inputs are finite; a program needn't handle non-finite values.
Results may differ from the reference program's by a relative error of at most 0.0071.
Values may be sent and summed in bfloat16 or wider, within the bound.
No kernel may reach another device: no remote copies, remote signals or barrier semaphores. Data moves between devices by JAX's collectives and lax.ppermute only.
A program may use at most 192 MiB of HBM per device.

```python
import jax
import jax.numpy as jnp
from jax import lax

D = 1024
HEADS = 32
HEADDIM = 64
NSTATE = 128
CONV_WIDTH = 4
BLOCK = 128
SEQS_DEV = 4
TOK_DEV = 256
INNER = 2048
CONVDIM = 2304
PROJ = 4384
BUFFERS = 32
TOKENS = 8192


def draw_lengths(key, part):
    key = jax.random.fold_in(key, 7)
    key_total, key_share, key_full, key_slot = jax.random.split(key, 4)
    totals = jax.random.randint(key_total, (BUFFERS, 1), TOK_DEV // 4, TOK_DEV + 1)
    shares = jax.random.randint(key_share, (BUFFERS, SEQS_DEV), 1, 17)
    running = jnp.cumsum(shares, axis=1).astype(jnp.int32)
    spare = totals - SEQS_DEV
    marks = jnp.arange(1, SEQS_DEV + 1, dtype=jnp.int32)[None, :] + spare * running // running[:, SEQS_DEV - 1:]
    spans = jnp.diff(marks, axis=1, prepend=jnp.zeros((BUFFERS, 1), jnp.int32))
    full_row = jax.random.randint(key_full, (), 0, BUFFERS)
    long_slot = jax.random.randint(key_slot, (), 0, SEQS_DEV)
    slot_ids = jnp.arange(SEQS_DEV, dtype=jnp.int32)
    full_spans = jnp.where(slot_ids == long_slot, TOK_DEV - SEQS_DEV + 1, 1)
    row_ids = jnp.arange(BUFFERS, dtype=jnp.int32)[:, None]
    return jnp.where(row_ids == full_row, full_spans[None, :], spans).astype(jnp.int32)


def block_levels(rng, extent, cuts, low, high):
    loudness, own = 1.0, jax.random.fold_in(rng, 6)
    for position, blocks in cuts:
        steps = jnp.exp(jax.random.uniform(jax.random.fold_in(own, position), (blocks,), jnp.float32, low / len(cuts), high / len(cuts)))
        loudness = loudness * jnp.repeat(steps, extent[position] // blocks).reshape([-1 if axis == position else 1 for axis in range(len(extent))])
    return loudness


def centred(stream_key, extent, scale, reach, cuts=(), held_as=jnp.bfloat16):
    entries = scale * jax.random.normal(stream_key, extent, jnp.float32)
    if cuts:
        entries = entries * block_levels(stream_key, extent, cuts, -0.22, 0.18)
    return jnp.clip(entries, -reach, reach).astype(held_as)


def setup_inputs(seed: int = 0) -> dict:
    splits = jax.random.split(jax.random.key(seed), 13)
    return {
        "tokens": centred(splits[0], (TOKENS, D), 1.0, 6.0, ((0, 32),)),
        "lengths": draw_lengths(jax.random.fold_in(splits[12], 71), 0),
        "norm_gain": jnp.clip(1.0 + 0.18 * jax.random.normal(splits[2], (D,), jnp.float32), 0.099609375, 1.8984375).astype(jnp.bfloat16),
        "in_weight": centred(splits[3], (D, PROJ), D ** -0.5, 0.1875, ((0, 2),)),
        "conv_weight": centred(splits[4], (CONVDIM, CONV_WIDTH), 0.5, 3.0, ((0, 2),)),
        "conv_bias": centred(splits[5], (CONVDIM,), 0.5, 3.0, ((0, 2),)),
        "step_bias": jnp.clip(-7.0 + 4.5 * jax.random.uniform(splits[6], (HEADS,), jnp.float32) ** block_levels(splits[6], (HEADS,), ((0, 2),), -0.2, 0.2), -7.0, -2.5).astype(jnp.bfloat16),
        "decay_log": jnp.clip(2.796875 * jax.random.uniform(splits[7], (HEADS,), jnp.float32) ** block_levels(splits[7], (HEADS,), ((0, 2),), -0.2, 0.2), 0.0, 2.796875).astype(jnp.bfloat16),
        "skip_gain": jnp.clip(0.5 + 1.5 * jax.random.uniform(splits[8], (HEADS,), jnp.float32) ** block_levels(splits[8], (HEADS,), ((0, 2),), -0.2, 0.2), 0.5, 2.0).astype(jnp.bfloat16),
        "gate_gain": jnp.clip(1.0 + 0.18 * jax.random.normal(splits[9], (INNER,), jnp.float32), 0.099609375, 1.8984375).astype(jnp.bfloat16),
        "out_weight": centred(splits[10], (INNER, D), INNER ** -0.5, 0.125, ((0, 2),)),
        "cotangent": centred(splits[11], (TOKENS, D), 1.0, 6.0, ((0, 32),)),
    }


epsilon = 1e-05
highest = lax.Precision.HIGHEST

@jax.custom_vjp
def low(v):
    return lax.optimization_barrier(v.astype(jnp.bfloat16)).astype(jnp.float32)

@jax.custom_vjp
def low_back(v):
    return v

def low_keep(v):
    return (low(v), None)

def low_pass(kept, grad):
    return (grad,)

def back_keep(v):
    return (v, None)

def back_low(kept, grad):
    return (low(grad),)
low.defvjp(low_keep, low_pass)
low_back.defvjp(back_keep, back_low)

def rms_scale(values, gain):
    return values * lax.rsqrt(lax.optimization_barrier(jnp.mean(values * values, axis=-1, keepdims=True)) + epsilon) * gain

def segment_ids(seq_lengths, length_rows):
    seq_ends = jnp.cumsum(seq_lengths).astype(jnp.int32)
    places = jnp.arange(length_rows, dtype=jnp.int32)
    return lax.optimization_barrier(jnp.sum((places[:, None] >= seq_ends[None, :]).astype(jnp.int32), axis=1)).astype(jnp.int32)

def causal_conv(signal, segment, kernel_taps, kernel_bias):
    summed = kernel_bias[None, :] + signal * kernel_taps[:, CONV_WIDTH - 1][None, :]
    for offset in range(1, CONV_WIDTH):
        shifted = jnp.concatenate([jnp.zeros((offset, signal.shape[1]), signal.dtype), signal[:-offset]], axis=0)
        earlier = jnp.concatenate([jnp.full((offset,), -1, jnp.int32), segment[:-offset]])
        joined = (earlier == segment).astype(signal.dtype)
        summed = summed + shifted * joined[:, None] * kernel_taps[:, CONV_WIDTH - 1 - offset][None, :]
    return summed

def block_step(carry, pieces):
    memory, prior_segment = carry
    head_input, write_map, read_map, step_size, log_decay, segment = pieces
    block_rows = read_map.shape[0]
    running = jnp.cumsum(log_decay, axis=0)
    head_major = running.T
    places = jnp.arange(block_rows, dtype=jnp.int32)
    linked = (segment[:, None] == segment[None, :]) & (places[:, None] >= places[None, :])
    spread = head_major[:, :, None] - head_major[:, None, :]
    decays = jnp.exp(jnp.where(linked[None], spread, -1e+30))
    scores = jnp.dot(read_map, write_map.T, precision=highest)
    mixing = decays * scores[None] * step_size.T[:, None, :]
    within = jnp.einsum('hij,jhp->ihp', mixing, head_input, precision=highest)
    joined = (segment == prior_segment).astype(read_map.dtype)
    carried = jnp.einsum('in,hpn->ihp', read_map, memory, precision=highest)
    carried = carried * (jnp.exp(running) * joined[:, None])[:, :, None]
    last_segment = segment[block_rows - 1]
    toward_end = jnp.exp(running[block_rows - 1][None, :] - running)
    toward_end = toward_end * (segment == last_segment).astype(read_map.dtype)[:, None] * step_size
    weighted = head_input * toward_end[:, :, None]
    fresh_state = jnp.einsum('jn,jhp->hpn', write_map, weighted, precision=highest)
    passed = memory * jnp.where(last_segment == prior_segment, jnp.exp(running[block_rows - 1]), 0.0)[:, None, None]
    return ((passed + fresh_state, last_segment), within + carried)

def state_space(head_input, write_map, read_map, step_size, log_decay, segment):
    token_rows = read_map.shape[0]
    block_count = token_rows // BLOCK
    pieces = (head_input.reshape(block_count, BLOCK, HEADS, HEADDIM), write_map.reshape(block_count, BLOCK, NSTATE), read_map.reshape(block_count, BLOCK, NSTATE), step_size.reshape(block_count, BLOCK, HEADS), log_decay.reshape(block_count, BLOCK, HEADS), segment.reshape(block_count, BLOCK))
    initial = (jnp.zeros((HEADS, HEADDIM, NSTATE), read_map.dtype), jnp.array(-1, jnp.int32))
    unused, results = lax.scan(jax.checkpoint(block_step), initial, pieces)
    return results.reshape(token_rows, HEADS, HEADDIM)

def mixer_block(projected, segment, kernel_taps, kernel_bias, step_offset, decay_rates, skip_terms, gate_scale):
    gate_part = projected[:, :INNER]
    signal = projected[:, INNER:INNER + CONVDIM]
    step_raw = projected[:, INNER + CONVDIM:]
    activated = jax.nn.silu(causal_conv(signal, segment, kernel_taps, kernel_bias))
    head_input = activated[:, :INNER].reshape(-1, HEADS, HEADDIM)
    write_map = activated[:, INNER:INNER + NSTATE]
    read_map = activated[:, INNER + NSTATE:]
    step_size = jax.nn.softplus(step_raw + step_offset[None, :])
    log_decay = -step_size * jnp.exp(decay_rates)[None, :]
    heads_out = state_space(head_input, write_map, read_map, step_size, log_decay, segment)
    heads_out = heads_out + skip_terms[None, :, None] * head_input
    gated_in = heads_out.reshape(-1, INNER) * jax.nn.silu(gate_part)
    return rms_scale(gated_in, gate_scale)

def layer_block(inputs, segment, live, norm_gain, in_weight, conv_weight, conv_bias, step_bias, decay_log, skip_gain, gate_gain, out_weight):
    normed = low(rms_scale(inputs, norm_gain))
    projected = low_back(jnp.dot(normed, in_weight, precision=highest))
    gated_out = low(mixer_block(projected, segment, conv_weight, conv_bias, step_bias, decay_log, skip_gain, gate_gain))
    return inputs + live[:, None] * jnp.dot(gated_out, out_weight, precision=highest)

def reference(tokens, lengths, norm_gain, in_weight, conv_weight, conv_bias, step_bias, decay_log, skip_gain, gate_gain, out_weight, cotangent):
    weights = tuple((member.astype(jnp.float32) for member in (norm_gain, in_weight, conv_weight, conv_bias, step_bias, decay_log, skip_gain, gate_gain, out_weight)))

    def visit_buffer(totals, buffer):
        inputs, seq_lengths, upstream = buffer
        segment = segment_ids(seq_lengths, TOK_DEV)
        live = (segment < SEQS_DEV).astype(jnp.float32)

        def forward(inputs, *params):
            return layer_block(inputs, segment, live, *params)
        result, backward = jax.vjp(forward, inputs.astype(jnp.float32), *weights)
        gradients = backward(upstream.astype(jnp.float32))
        totals = tuple((left_sum + right_sum for left_sum, right_sum in zip(totals, gradients[1:])))
        return (totals, (result.astype(jnp.bfloat16), gradients[0]))
    initial = tuple((jnp.zeros(member.shape, jnp.float32) for member in weights))
    buffers = (tokens.reshape(BUFFERS, TOK_DEV, D), lengths, cotangent.reshape(BUFFERS, TOK_DEV, D))
    totals, (outputs, input_grads) = lax.scan(visit_buffer, initial, buffers)
    return (outputs.reshape(TOKENS, D), input_grads.reshape(TOKENS, D), totals[0], totals[1], totals[2], totals[3], totals[4], totals[5], totals[6], totals[7], totals[8])
```

```python
import jax
import jax.numpy as jnp
from jax import lax
from jax.experimental import pallas as pl
from jax.experimental.pallas import tpu as pltpu
from jax.sharding import PartitionSpec as P

HEADS = 32
HEADDIM = 64
NSTATE = 128
CONV_WIDTH = 4
BLOCK = 128
INNER = 2048
CONVDIM = 2304
STEP_COL = INNER + CONVDIM

GROUP = 4
WIDE = GROUP * HEADDIM
STEPS = HEADS // GROUP
LANES = 128

epsilon = 1e-05
highest = lax.Precision.HIGHEST
f32 = jnp.float32
bf16 = jnp.bfloat16


def mm(left, right, dims=((1,), (0,)), precision=None):
    return lax.dot_general(left, right, (dims, ((), ())), precision=precision, preferred_element_type=f32)


LANE = ((1,), (1,))
ROWS = ((0,), (0,))


def segment_of(places, len_ref):
    end = len_ref[0, 0]
    segment = (places >= end).astype(jnp.int32)
    for slot in range(1, len_ref.shape[1]):
        end = end + len_ref[0, slot]
        segment = segment + (places >= end).astype(jnp.int32)
    return segment


def write_joined(len_ref, joined_ref):
    rows, lanes = joined_ref.shape[1:]
    places = lax.broadcasted_iota(jnp.int32, (rows, lanes), 0)
    segment = segment_of(places, len_ref)
    for offset in range(1, CONV_WIDTH):
        same = (segment_of(places - offset, len_ref) == segment) & (places >= offset)
        joined_ref[offset - 1] = same.astype(f32)


def wide(mask):
    return jnp.concatenate([mask, mask], axis=1)


def linked(len_ref, row_start, col_start):
    rows = lax.broadcasted_iota(jnp.int32, (BLOCK, BLOCK), 0) + row_start
    cols = lax.broadcasted_iota(jnp.int32, (BLOCK, BLOCK), 1) + col_start
    return (segment_of(rows, len_ref) == segment_of(cols, len_ref)) & (rows >= cols)


def step_terms(raw_ref, head_ref):
    lane = lax.broadcasted_iota(jnp.int32, raw_ref.shape, 1)
    shifted = jnp.where(lane < HEADS, raw_ref[...] + head_ref[0:1, :], 0.0)
    step = jnp.maximum(shifted, 0.0) + jnp.log1p(jnp.exp(-jnp.abs(shifted)))
    rate = jnp.exp(head_ref[1:2, :])
    return shifted, step, rate, -step * rate


def lower():
    rows = lax.broadcasted_iota(jnp.int32, (BLOCK, BLOCK), 0)
    cols = lax.broadcasted_iota(jnp.int32, (BLOCK, BLOCK), 1)
    return (rows >= cols).astype(f32)


def write_running(raw_ref, head_ref, step_ref, run_ref, runt_ref):
    unused, step, rate, decay = step_terms(raw_ref, head_ref)
    step_ref[...] = step
    for block in range(2):
        rows = slice(block * BLOCK, (block + 1) * BLOCK)
        running = mm(lower(), decay[rows], precision=highest)
        run_ref[rows, :] = running
        turned = running.T
        for group in range(STEPS):
            runt_ref[group, 0:GROUP, rows] = turned[group * GROUP : (group + 1) * GROUP]


def conv_silu(signal, par, joined_ref):
    summed = par[4:5] + signal * par[3:4]
    for offset in range(1, CONV_WIDTH):
        tap = par[3 - offset : 4 - offset]
        summed = summed + pltpu.roll(signal, offset, 0) * wide(joined_ref[offset - 1]) * tap
    return summed


def conv_back(grad, signal, par, joined_ref, store):
    rows = grad.shape[0]
    back = grad * par[3:4]
    store(3, jnp.sum(grad * signal, axis=0, keepdims=True))
    store(4, jnp.sum(grad, axis=0, keepdims=True))
    for offset in range(1, CONV_WIDTH):
        masked = grad * wide(joined_ref[offset - 1])
        store(3 - offset, jnp.sum(masked * pltpu.roll(signal, offset, 0), axis=0, keepdims=True))
        back = back + pltpu.roll(masked, rows - offset, 0) * par[3 - offset : 4 - offset]
    return back


def logistic(value):
    return 1.0 / (1.0 + jnp.exp(-value))


def head_columns(table, step):
    return pltpu.roll(table, lax.rem(LANES - GROUP * step, LANES), 1)


def spread(columns, head):
    return jnp.broadcast_to(columns[:, head : head + 1], (columns.shape[0], LANES))


def half_lanes(shape):
    return lax.broadcasted_iota(jnp.int32, shape, 1) < HEADDIM


def decay_pair(pair, block, runs, runt_ref, step):
    rows = slice(block * BLOCK, (block + 1) * BLOCK)
    out = []
    for place in (2 * pair, 2 * pair + 1):
        row = runt_ref[step, place : place + 1, rows]
        out.append(jnp.exp(jnp.minimum(runs[place][rows] - row, 0.0)))
    return out


def split_heads(value):
    first = half_lanes(value.shape)
    zero = jnp.zeros_like(value)
    return jnp.concatenate([jnp.where(first, value, zero), jnp.where(first, zero, value)], axis=0)


def pair_terms(pair, runs, steps):
    first = half_lanes(runs[0].shape)
    run = jnp.where(first, runs[2 * pair], runs[2 * pair + 1])
    step = jnp.where(first, steps[2 * pair], steps[2 * pair + 1])
    into = jnp.exp(run[BLOCK:])
    toward = jnp.exp(run[BLOCK - 1 : BLOCK] - run[:BLOCK])
    return step, into, toward


def forward_kernel(
    len_ref, raw_ref, head_ref, sig_ref, bc_ref, gate_ref, grad_ref, par_ref, parbc_ref, gain_ref,
    gated_ref, dgate_ref, dheads_ref, heads_ref, conv_ref, convbc_ref, gaing_ref,
    joined, step_s, run_s, runt_s, score_s, cross_s, u_s, silu_s, slope_s, grad_s, sq_s, mix_s,
):
    step = pl.program_id(0)

    @pl.when(step == 0)
    def prepare():
        write_joined(len_ref, joined)
        write_running(raw_ref, head_ref, step_s, run_s, runt_s)
        summed = conv_silu(bc_ref[...], parbc_ref[...], joined)
        convbc_ref[...] = summed
        active = summed * logistic(summed)
        write_map, read_map = active[:, :NSTATE], active[:, NSTATE:]
        for block in range(2):
            rows = slice(block * BLOCK, (block + 1) * BLOCK)
            scores = mm(read_map[rows], write_map[rows], LANE, highest)
            score_s[block] = jnp.where(linked(len_ref, block * BLOCK, block * BLOCK), scores, 0.0)
        cross = mm(read_map[BLOCK:], write_map[:BLOCK], LANE, highest)
        cross_s[...] = jnp.where(linked(len_ref, BLOCK, 0), cross, 0.0).astype(bf16)
        sq_s[...] = jnp.zeros_like(sq_s)
        mix_s[...] = jnp.zeros_like(mix_s)

    par = par_ref[...]
    summed = conv_silu(sig_ref[...], par, joined)
    conv_ref[...] = summed
    head_in = summed * logistic(summed)
    run_cols = head_columns(run_s[...], step)
    step_cols = head_columns(step_s[...], step)
    runs = [spread(run_cols, head) for head in range(GROUP)]
    steps = [spread(step_cols, head) for head in range(GROUP)]
    tops, bottoms, intos, sources = [], [], [], []
    for pair in range(GROUP // 2):
        lanes = slice(pair * LANES, (pair + 1) * LANES)
        step_size, into, toward = pair_terms(pair, runs, steps)
        scaled = head_in[:, lanes] * step_size
        low = scaled.astype(bf16)
        for block, found in ((0, tops), (1, bottoms)):
            rows = slice(block * BLOCK, (block + 1) * BLOCK)
            first, second = decay_pair(pair, block, runs, runt_s, step)
            mixing = jnp.concatenate([first * score_s[block], second * score_s[block]], axis=1)
            found.append(mm(mixing.astype(bf16), split_heads(low[rows])))
        intos.append(into)
        sources.append((scaled[:BLOCK] * toward).astype(bf16))
    carried = mm(cross_s[...], jnp.concatenate(sources, axis=1)) * jnp.concatenate(intos, axis=1)
    top, bottom = jnp.concatenate(tops, axis=1), jnp.concatenate(bottoms, axis=1)
    heads_ref[:BLOCK] = top
    heads_ref[BLOCK:] = bottom
    heads = jnp.concatenate([top, bottom + carried], axis=0) + par[6:7] * head_in
    gate = gate_ref[...]
    opened = logistic(gate)
    silu = gate * opened
    u = heads * silu
    grad = grad_ref[...]
    mixed = grad * par[5:6] * u
    square = u * u
    sq_s[...] += square[:, :LANES] + square[:, LANES:]
    mix_s[...] += mixed[:, :LANES] + mixed[:, LANES:]
    u_s[step] = u
    silu_s[step] = silu
    slope_s[step] = heads * (opened * (1.0 + gate * (1.0 - opened)))
    grad_s[step] = grad

    @pl.when(step == STEPS - 1)
    def finish():
        scale = lax.rsqrt(jnp.sum(sq_s[...], axis=1, keepdims=True) * (1.0 / INNER) + epsilon)
        drag = scale * scale * scale * (jnp.sum(mix_s[...], axis=1, keepdims=True) * (1.0 / INNER))
        for part in range(STEPS):
            lanes = slice(part * WIDE, (part + 1) * WIDE)
            gain = gain_ref[:, lanes]
            normal = u_s[part] * scale
            grad = grad_s[part]
            gated_ref[:, lanes] = (normal * gain).astype(bf16)
            gaing_ref[:, lanes] = jnp.sum(grad * normal, axis=0, keepdims=True)
            du = scale * (grad * gain) - u_s[part] * drag
            dheads_ref[:, lanes] = du * silu_s[part]
            dgate_ref[:, lanes] = (du * slope_s[part]).astype(bf16)


def backward_kernel(
    len_ref, raw_ref, head_ref, sig_ref, bc_ref, conv_ref, convbc_ref, dheads_ref, heads_ref, par_ref, parbc_ref,
    dx_ref, dr_ref, parg_ref, parbcg_ref, headg_ref,
    joined, step_s, run_s, runt_s, maps_s, score_s, cross_s, dscore_s, dcross_s, dstep_s, ddecay_s,
):
    step = pl.program_id(0)

    @pl.when(step == 0)
    def prepare():
        write_joined(len_ref, joined)
        write_running(raw_ref, head_ref, step_s, run_s, runt_s)
        summed = convbc_ref[...]
        active = summed * logistic(summed)
        maps_s[...] = active
        write_map, read_map = active[:, :NSTATE], active[:, NSTATE:]
        for block in range(2):
            rows = slice(block * BLOCK, (block + 1) * BLOCK)
            scores = mm(read_map[rows], write_map[rows], LANE, highest)
            score_s[block] = jnp.where(linked(len_ref, block * BLOCK, block * BLOCK), scores, 0.0)
        cross = mm(read_map[BLOCK:], write_map[:BLOCK], LANE, highest)
        cross_s[...] = jnp.where(linked(len_ref, BLOCK, 0), cross, 0.0).astype(bf16)
        dscore_s[...] = jnp.zeros_like(dscore_s)
        dcross_s[...] = jnp.zeros_like(dcross_s)
        dstep_s[...] = jnp.zeros_like(dstep_s)
        ddecay_s[...] = jnp.zeros_like(ddecay_s)

    par = par_ref[...]
    summed = conv_ref[...]
    opened = logistic(summed)
    head_in = summed * opened
    slope = opened * (1.0 + summed * (1.0 - opened))
    run_cols = head_columns(run_s[...], step)
    step_cols = head_columns(step_s[...], step)
    runs = [spread(run_cols, head) for head in range(GROUP)]
    steps = [spread(step_cols, head) for head in range(GROUP)]
    dheads = dheads_ref[...]
    dlow = dheads.astype(bf16)
    tops, bottoms, towards, sinks, sources, lows, sizes = [], [], [], [], [], [], []
    for pair in range(GROUP // 2):
        lanes = slice(pair * LANES, (pair + 1) * LANES)
        step_size, into, toward = pair_terms(pair, runs, steps)
        scaled = head_in[:, lanes] * step_size
        low = scaled.astype(bf16)
        for block, found in ((0, tops), (1, bottoms)):
            rows = slice(block * BLOCK, (block + 1) * BLOCK)
            first, second = decay_pair(pair, block, runs, runt_s, step)
            mixing = jnp.concatenate([first * score_s[block], second * score_s[block]], axis=0)
            parted = split_heads(dlow[rows, lanes])
            found.append(mm(mixing.astype(bf16), parted, ROWS))
            dmixing = mm(parted, low[rows], LANE)
            dscore_s[block] += first * dmixing[:BLOCK] + second * dmixing[BLOCK:]
        sinks.append((dheads[BLOCK:, lanes] * into).astype(bf16))
        sources.append((scaled[:BLOCK] * toward).astype(bf16))
        towards.append(toward)
        lows.append(low)
        sizes.append(step_size)
    sink, source = jnp.concatenate(sinks, axis=1), jnp.concatenate(sources, axis=1)
    dcross_s[...] += mm(sink, source, LANE)
    arrived, returned = mm(cross_s[...], source), mm(cross_s[...], sink, ROWS)
    inside = jnp.concatenate([jnp.concatenate(tops, axis=1), jnp.concatenate(bottoms, axis=1)], axis=0)
    dscaled = jnp.concatenate(
        [inside[:BLOCK] + returned * jnp.concatenate(towards, axis=1), inside[BLOCK:]], axis=0
    )
    between = jnp.concatenate([-source.astype(f32) * returned, sink.astype(f32) * arrived], axis=0)
    owner = lax.broadcasted_iota(jnp.int32, (WIDE, LANES), 0) // HEADDIM + GROUP * step
    sums = (owner == lax.broadcasted_iota(jnp.int32, (WIDE, LANES), 1)).astype(f32)
    low = jnp.concatenate(lows, axis=1).astype(f32)
    moved = dlow.astype(f32) * heads_ref[...] - low * inside + between
    ddecay_s[...] += mm(moved, sums, precision=highest)
    dstep_s[...] += mm(head_in * dscaled, sums, precision=highest)
    dhead_in = jnp.concatenate(sizes, axis=1) * dscaled + par[6:7] * dheads

    def store(row, value):
        parg_ref[row : row + 1, :] = value

    store(5, jnp.zeros((1, WIDE), f32))
    store(6, jnp.sum(dheads * head_in, axis=0, keepdims=True))
    store(7, jnp.zeros((1, WIDE), f32))
    dx_ref[...] = conv_back(dhead_in * slope, sig_ref[...], par, joined, store).astype(bf16)

    @pl.when(step == STEPS - 1)
    def finish():
        maps = maps_s[...]
        write_map, read_map = maps[:, :NSTATE], maps[:, NSTATE:]
        w0, w1, r0, r1 = write_map[:BLOCK], write_map[BLOCK:], read_map[:BLOCK], read_map[BLOCK:]
        d0 = jnp.where(linked(len_ref, 0, 0), dscore_s[0], 0.0)
        d1 = jnp.where(linked(len_ref, BLOCK, BLOCK), dscore_s[1], 0.0)
        dc = jnp.where(linked(len_ref, BLOCK, 0), dcross_s[...], 0.0)
        dread = jnp.concatenate(
            [mm(d0, w0, precision=highest), mm(d1, w1, precision=highest) + mm(dc, w0, precision=highest)], axis=0
        )
        dwrite = jnp.concatenate(
            [mm(d0, r0, ROWS, highest) + mm(dc, r1, ROWS, highest), mm(d1, r1, ROWS, highest)], axis=0
        )
        summed = convbc_ref[...]
        opened = logistic(summed)
        slope = opened * (1.0 + summed * (1.0 - opened))

        def store(row, value):
            parbcg_ref[row : row + 1, :] = value

        for row in (5, 6, 7):
            store(row, jnp.zeros((1, WIDE), f32))
        grad = jnp.concatenate([dwrite, dread], axis=1) * slope
        dr_ref[:, :WIDE] = conv_back(grad, bc_ref[...], parbc_ref[...], joined, store).astype(bf16)

        shifted, step_size, rate, decay = step_terms(raw_ref, head_ref)
        change = ddecay_s[...]
        late = mm(lower(), change[BLOCK:], ROWS, highest)
        early = mm(lower(), change[:BLOCK], ROWS, highest) + late[0:1]
        ddecay = jnp.concatenate([early, late], axis=0)
        dshifted = (dstep_s[...] - rate * ddecay) * logistic(shifted)
        lane = lax.broadcasted_iota(jnp.int32, dshifted.shape, 1)
        dshifted = jnp.where(lane < HEADS, dshifted, 0.0)
        dr_ref[:, WIDE:] = dshifted.astype(bf16)
        headg_ref[...] = jnp.zeros_like(headg_ref)
        headg_ref[0:1, :] = jnp.sum(dshifted, axis=0, keepdims=True)
        headg_ref[1:2, :] = jnp.sum(decay * ddecay, axis=0, keepdims=True)


def whole(shape):
    return pl.BlockSpec(shape, lambda step: (0,) * len(shape))


def columns(rows, start=0):
    return pl.BlockSpec((rows, WIDE), lambda step: (0, start + step))


def fixed_columns(rows, start):
    return pl.BlockSpec((rows, WIDE), lambda step: (0, start))


def shape(rows, cols, dtype=f32):
    return jax.ShapeDtypeStruct((rows, cols), dtype)


def params():
    return pltpu.CompilerParams(dimension_semantics=("arbitrary",), vmem_limit_bytes=48 * 1024 * 1024)


def run_forward(lengths, raw, head, projected, gated_grad, par, gain):
    rows = projected.shape[0]
    state = pltpu.VMEM((STEPS, rows, WIDE), f32)
    narrow = pltpu.VMEM((rows, LANES), f32)
    return pl.pallas_call(
        forward_kernel,
        grid=(STEPS,),
        in_specs=[
            pl.BlockSpec(memory_space=pltpu.SMEM),
            whole((rows, LANES)),
            whole((8, LANES)),
            columns(rows, INNER // WIDE),
            fixed_columns(rows, 2 * INNER // WIDE),
            columns(rows),
            columns(rows),
            columns(8),
            fixed_columns(8, INNER // WIDE),
            whole((1, INNER)),
        ],
        out_specs=[
            whole((rows, INNER)), whole((rows, INNER)), whole((rows, INNER)),
            columns(rows), columns(rows), whole((rows, WIDE)), whole((1, INNER)),
        ],
        out_shape=[
            shape(rows, INNER, bf16), shape(rows, INNER, bf16), shape(rows, INNER),
            shape(rows, INNER), shape(rows, INNER), shape(rows, WIDE), shape(1, INNER),
        ],
        scratch_shapes=[
            pltpu.VMEM((CONV_WIDTH - 1, rows, LANES), f32),
            narrow, narrow, pltpu.VMEM((STEPS, 8, rows), f32),
            pltpu.VMEM((2, BLOCK, BLOCK), f32), pltpu.VMEM((BLOCK, BLOCK), bf16),
            state, state, state, state, narrow, narrow,
        ],
        compiler_params=params(),
        cost_estimate=pl.CostEstimate(flops=600_000_000, bytes_accessed=16_000_000, transcendentals=3_000_000),
        name="mixer_forward",
    )(lengths, raw, head, projected, projected, projected, gated_grad, par, par, gain)


def run_backward(lengths, raw, head, projected, conv, convbc, dheads, heads, par):
    rows = projected.shape[0]
    narrow = pltpu.VMEM((rows, LANES), f32)
    square = pltpu.VMEM((2, BLOCK, BLOCK), f32)
    return pl.pallas_call(
        backward_kernel,
        grid=(STEPS,),
        in_specs=[
            pl.BlockSpec(memory_space=pltpu.SMEM),
            whole((rows, LANES)),
            whole((8, LANES)),
            columns(rows, INNER // WIDE),
            fixed_columns(rows, 2 * INNER // WIDE),
            columns(rows), whole((rows, WIDE)), columns(rows), columns(rows),
            columns(8),
            fixed_columns(8, INNER // WIDE),
        ],
        out_specs=[
            columns(rows), whole((rows, WIDE + LANES)), columns(8), whole((8, WIDE)), whole((8, LANES)),
        ],
        out_shape=[
            shape(rows, INNER, bf16), shape(rows, WIDE + LANES, bf16), shape(8, INNER), shape(8, WIDE), shape(8, LANES),
        ],
        scratch_shapes=[
            pltpu.VMEM((CONV_WIDTH - 1, rows, LANES), f32),
            narrow, narrow, pltpu.VMEM((STEPS, 8, rows), f32), pltpu.VMEM((rows, WIDE), f32),
            square, pltpu.VMEM((BLOCK, BLOCK), bf16), square, pltpu.VMEM((BLOCK, BLOCK), f32), narrow, narrow,
        ],
        compiler_params=params(),
        cost_estimate=pl.CostEstimate(flops=1_500_000_000, bytes_accessed=16_000_000, transcendentals=3_000_000),
        name="mixer_backward",
    )(lengths, raw, head, projected, projected, conv, convbc, dheads, heads, par, par)


def make_shards(mesh):
    reps = mesh.shape["rep"]
    bits = reps.bit_length() - 1
    assert reps == 1 << bits and mesh.shape["shard"] == 2
    one_way = tuple(range(bits))
    turn = bits // 4 if bits >= 4 else min(1, bits)
    other_way = one_way[turn : 2 * turn] + one_way[:turn] + one_way[2 * turn :]

    def swap(value):
        return lax.ppermute(value, "shard", [(0, 1), (1, 0)])

    def across(value, bit):
        return lax.ppermute(value, "rep", [(place, place ^ (1 << bit)) for place in range(reps)])

    def scatter_sum(value, order):
        for bit in order:
            half = value.shape[0] // 2
            side = (lax.axis_index("rep") >> bit) & 1
            leaving = lax.dynamic_slice_in_dim(value, (1 - side) * half, half).astype(bf16)
            kept = lax.dynamic_slice_in_dim(value, side * half, half)
            value = kept + across(leaving, bit).astype(f32)
        return value.astype(bf16)

    def gather(value, order):
        for bit in reversed(order):
            side = (lax.axis_index("rep") >> bit) & 1
            value = joined(side, value, across(value, bit), 0)
        return value

    def joined(side, mine, theirs, axis):
        return jnp.where(
            side == 0, jnp.concatenate([mine, theirs], axis=axis), jnp.concatenate([theirs, mine], axis=axis)
        )

    def summed_over_reps(value):
        half = value.shape[0] // 2
        return jnp.concatenate(
            [
                gather(scatter_sum(value[:half], one_way), one_way),
                gather(scatter_sum(value[half:], other_way), other_way),
            ],
            axis=0,
        ).astype(f32)

    def shards(
        tokens, lengths, norm_gain, in_weight, conv_weight, conv_bias, step_bias, decay_log, skip_gain,
        gate_gain, out_weight, cotangent,
    ):
        core = lax.axis_index("shard")
        rows, model = tokens.shape
        half_model, half_inner = model // 2, INNER // 2
        half_conv, half_heads = CONVDIM // 2, HEADS // 2

        def mine(value, size):
            return lax.dynamic_slice_in_dim(value, core * size, size, axis=1)

        def theirs(value, size):
            return lax.dynamic_slice_in_dim(value, (1 - core) * size, size, axis=1)

        def line(value):
            return jnp.pad(value, (0, half_conv - value.shape[0]))[None]

        small = jnp.concatenate(
            [
                conv_weight.T, conv_bias[None], line(gate_gain),
                line(jnp.concatenate([norm_gain, step_bias, decay_log, skip_gain])),
                jnp.zeros((1, half_conv), bf16),
            ],
            axis=0,
        )
        small_o = swap(small)
        in_other = swap(in_weight)
        out_other = swap(out_weight)
        small, small_o = small.astype(f32), small_o.astype(f32)
        low_half, high_half = jnp.where(core == 0, small, small_o), jnp.where(core == 0, small_o, small)
        both = jnp.concatenate([low_half, high_half], axis=1)

        def pick(row, start, size):
            return jnp.concatenate([low_half[row, start : start + size], high_half[row, start : start + size]])

        norm_scale = pick(6, 0, half_model)
        head_lines = [pick(6, half_model + at * half_heads, half_heads) for at in range(3)]
        gate_line = pick(5, 0, half_inner)[None]
        par = jnp.concatenate(
            [
                both[:5],
                jnp.pad(gate_line, ((0, 0), (0, CONVDIM - INNER))),
                jnp.pad(jnp.repeat(head_lines[2], HEADDIM)[None], ((0, 0), (0, CONVDIM - INNER))),
                jnp.zeros((1, CONVDIM), f32),
            ],
            axis=0,
        )
        head = jnp.pad(jnp.stack(head_lines[:2]), ((0, 6), (0, LANES - HEADS)))

        live = (jnp.arange(rows, dtype=jnp.int32) < jnp.sum(lengths))[:, None]
        upstream = jnp.where(live, cotangent, jnp.zeros_like(cotangent))
        up_pair = jnp.concatenate([upstream, swap(upstream)], axis=0)
        inputs = tokens.astype(f32)
        scale = lax.rsqrt(jnp.mean(inputs * inputs, axis=-1, keepdims=True) + epsilon)
        normed = (inputs * scale * norm_scale).astype(bf16)
        normed_m, normed_o = mine(normed, half_model), theirs(normed, half_model)
        normed_pair = jnp.concatenate([normed_m, swap(normed_o)], axis=0)

        gated_grad = joined(core, mm(upstream, out_weight, LANE), mm(upstream, out_other, LANE), 1)
        projected = mm(normed_m, in_weight) + mm(normed_o, in_other)
        raw = jnp.pad(projected[:, STEP_COL:], ((0, 0), (0, LANES - HEADS)))
        gated, dgate, dheads, heads, conv, convbc, gain_g = run_forward(
            lengths, raw, head, projected, gated_grad, par, gate_line
        )

        def pair_of(value):
            return jnp.concatenate([value, swap(value)], axis=0)

        gated_m, gated_o = mine(gated, half_inner), theirs(gated, half_inner)
        gated_pair = jnp.concatenate([gated_m, swap(gated_o)], axis=0)
        out_grad = summed_over_reps(mm(gated_pair, up_pair, ROWS))
        gate_grad = summed_over_reps(mm(normed_pair, pair_of(dgate), ROWS))
        branch = mm(gated_m, out_weight) + mm(gated_o, out_other)
        output = (inputs + jnp.where(live, branch, 0.0)).astype(bf16)

        dx, dr, par_g, parbc_g, head_g = run_backward(
            lengths, raw, head, projected, conv, convbc, dheads, heads, par
        )
        late = jnp.concatenate([dx, dr], axis=1)
        late_grad = summed_over_reps(mm(normed_pair, pair_of(late), ROWS))
        in_grad = jnp.concatenate([gate_grad, late_grad[:, : STEP_COL + HEADS - INNER]], axis=1)

        proj_grad = jnp.concatenate([dgate, late[:, : STEP_COL + HEADS - INNER]], axis=1)
        normed_grad = joined(core, mm(proj_grad, in_weight, LANE), mm(proj_grad, in_other, LANE), 1)
        g = normed_grad * norm_scale
        input_grad = (
            cotangent.astype(f32)
            + scale * g
            - inputs * (scale * scale * scale * jnp.mean(g * inputs, axis=-1, keepdims=True))
        )
        gain_grad = jnp.sum(normed_grad * inputs * scale, axis=0)

        skip_g = jnp.sum(par_g[6].reshape(HEADS, HEADDIM), axis=1)
        tail = jnp.concatenate([gain_grad, head_g[0, :HEADS], head_g[1, :HEADS], skip_g])
        total = jnp.concatenate(
            [
                jnp.concatenate([par_g[:5], parbc_g[:5]], axis=1),
                jnp.pad(gain_g, ((0, 0), (0, CONVDIM - INNER))),
                jnp.pad(tail, (0, CONVDIM - tail.shape[0]))[None],
                jnp.zeros((1, CONVDIM), f32),
            ],
            axis=0,
        )
        total = total + swap(total)
        for bit in one_way:
            total = total + across(total, bit)

        def own(row, start, size):
            return lax.dynamic_slice_in_dim(total[row], start + core * size, size)

        return (
            output,
            input_grad,
            own(6, 0, half_model),
            in_grad,
            lax.dynamic_slice_in_dim(total[:4], core * half_conv, half_conv, axis=1).T,
            own(4, 0, half_conv),
            own(6, model, half_heads),
            own(6, model + HEADS, half_heads),
            own(6, model + 2 * HEADS, half_heads),
            own(5, 0, half_inner),
            out_grad,
        )

    return shards


def solution(mesh):
    split = P(("rep", "shard"), None)
    vector, matrix = P("shard"), P("shard", None)
    in_specs = (
        split, split, vector, matrix, matrix, vector, vector, vector, vector, vector, matrix, split,
    )
    out_specs = (
        split, split, vector, matrix, matrix, vector, vector, vector, vector, vector, matrix,
    )
    return jax.shard_map(make_shards(mesh), mesh=mesh, in_specs=in_specs, out_specs=out_specs, check_vma=False)
```

```python
import jax
import jax.numpy as jnp
from jax import lax
from jax.experimental import pallas as pl
from jax.experimental.pallas import tpu as pltpu
from jax.sharding import PartitionSpec as P

HEADS = 32
HEADDIM = 64
NSTATE = 128
CONV_WIDTH = 4
BLOCK = 128
INNER = 2048
CONVDIM = 2304
STEP_COL = INNER + CONVDIM

GROUP = 4
WIDE = GROUP * HEADDIM
STEPS = HEADS // GROUP
QUARTERS = 4
LATE = INNER // QUARTERS + NSTATE
LANES = 128

epsilon = 1e-05
highest = lax.Precision.HIGHEST
f32 = jnp.float32
bf16 = jnp.bfloat16


def mm(left, right, dims=((1,), (0,)), precision=None):
    return lax.dot_general(left, right, (dims, ((), ())), precision=precision, preferred_element_type=f32)


LANE = ((1,), (1,))
ROWS = ((0,), (0,))


def segment_of(places, len_ref):
    end = len_ref[0, 0]
    segment = (places >= end).astype(jnp.int32)
    for slot in range(1, len_ref.shape[1]):
        end = end + len_ref[0, slot]
        segment = segment + (places >= end).astype(jnp.int32)
    return segment


def write_joined(len_ref, joined_ref):
    rows, lanes = joined_ref.shape[1:]
    places = lax.broadcasted_iota(jnp.int32, (rows, lanes), 0)
    segment = segment_of(places, len_ref)
    for offset in range(1, CONV_WIDTH):
        same = (segment_of(places - offset, len_ref) == segment) & (places >= offset)
        joined_ref[offset - 1] = same.astype(f32)


def wide(mask):
    return jnp.concatenate([mask, mask], axis=1)


def linked(len_ref, row_start, col_start):
    rows = lax.broadcasted_iota(jnp.int32, (BLOCK, BLOCK), 0) + row_start
    cols = lax.broadcasted_iota(jnp.int32, (BLOCK, BLOCK), 1) + col_start
    return (segment_of(rows, len_ref) == segment_of(cols, len_ref)) & (rows >= cols)


def step_terms(raw_ref, head_ref):
    lane = lax.broadcasted_iota(jnp.int32, raw_ref.shape, 1)
    shifted = jnp.where(lane < HEADS, raw_ref[...] + head_ref[0:1, :], 0.0)
    step = jnp.maximum(shifted, 0.0) + jnp.log1p(jnp.exp(-jnp.abs(shifted)))
    rate = jnp.exp(head_ref[1:2, :])
    return shifted, step, rate, -step * rate


def lower():
    rows = lax.broadcasted_iota(jnp.int32, (BLOCK, BLOCK), 0)
    cols = lax.broadcasted_iota(jnp.int32, (BLOCK, BLOCK), 1)
    return (rows >= cols).astype(f32)


def write_running(raw_ref, head_ref, step_ref, run_ref, runt_ref):
    unused, step, rate, decay = step_terms(raw_ref, head_ref)
    step_ref[...] = step
    for block in range(2):
        rows = slice(block * BLOCK, (block + 1) * BLOCK)
        running = mm(lower(), decay[rows], precision=highest)
        run_ref[rows, :] = running
        turned = running.T
        for group in range(STEPS):
            runt_ref[group, 0:GROUP, rows] = turned[group * GROUP : (group + 1) * GROUP]


def conv_silu(signal, par, joined_ref):
    summed = par[4:5] + signal * par[3:4]
    for offset in range(1, CONV_WIDTH):
        tap = par[3 - offset : 4 - offset]
        summed = summed + pltpu.roll(signal, offset, 0) * wide(joined_ref[offset - 1]) * tap
    return summed


def conv_back(grad, signal, par, joined_ref, store):
    rows = grad.shape[0]
    back = grad * par[3:4]
    store(3, jnp.sum(grad * signal, axis=0, keepdims=True))
    store(4, jnp.sum(grad, axis=0, keepdims=True))
    for offset in range(1, CONV_WIDTH):
        masked = grad * wide(joined_ref[offset - 1])
        store(3 - offset, jnp.sum(masked * pltpu.roll(signal, offset, 0), axis=0, keepdims=True))
        back = back + pltpu.roll(masked, rows - offset, 0) * par[3 - offset : 4 - offset]
    return back


def logistic(value):
    return 0.5 * jnp.tanh(0.5 * value) + 0.5


def head_columns(table, step):
    return pltpu.roll(table, lax.rem(LANES - GROUP * step, LANES), 1)


def spread(columns, head):
    return jnp.broadcast_to(columns[:, head : head + 1], (columns.shape[0], LANES))


def half_lanes(shape):
    return lax.broadcasted_iota(jnp.int32, shape, 1) < HEADDIM


def decay_pair(pair, block, runs, runt_ref, step):
    rows = slice(block * BLOCK, (block + 1) * BLOCK)
    out = []
    for place in (2 * pair, 2 * pair + 1):
        row = runt_ref[step, place : place + 1, rows]
        out.append(jnp.exp(jnp.minimum(runs[place][rows] - row, 0.0)))
    return out


def split_heads(value):
    first = half_lanes(value.shape)
    zero = jnp.zeros_like(value)
    return jnp.concatenate([jnp.where(first, value, zero), jnp.where(first, zero, value)], axis=0)


def pair_terms(pair, runs, steps):
    first = half_lanes(runs[0].shape)
    run = jnp.where(first, runs[2 * pair], runs[2 * pair + 1])
    step = jnp.where(first, steps[2 * pair], steps[2 * pair + 1])
    into = jnp.exp(run[BLOCK:])
    toward = jnp.exp(run[BLOCK - 1 : BLOCK] - run[:BLOCK])
    return step, into, toward


def forward_kernel(
    len_ref, raw_ref, head_ref, sig_ref, bc_ref, gate_ref, grad_ref, par_ref, parbc_ref, gain_ref,
    gated_ref, dgate_ref, sent_ref, dheads_ref, heads_ref, conv_ref, convbc_ref, gaing_ref,
    joined, step_s, run_s, runt_s, score_s, cross_s, u_s, silu_s, slope_s, grad_s, sq_s, mix_s,
):
    step = pl.program_id(0)

    @pl.when(step == 0)
    def prepare():
        write_joined(len_ref, joined)
        write_running(raw_ref, head_ref, step_s, run_s, runt_s)
        summed = conv_silu(bc_ref[...], parbc_ref[...], joined)
        convbc_ref[...] = summed
        active = summed * logistic(summed)
        write_map, read_map = active[:, :NSTATE], active[:, NSTATE:]
        for block in range(2):
            rows = slice(block * BLOCK, (block + 1) * BLOCK)
            scores = mm(read_map[rows], write_map[rows], LANE, highest)
            score_s[block] = jnp.where(linked(len_ref, block * BLOCK, block * BLOCK), scores, 0.0)
        cross = mm(read_map[BLOCK:], write_map[:BLOCK], LANE, highest)
        cross_s[...] = jnp.where(linked(len_ref, BLOCK, 0), cross, 0.0).astype(bf16)
        sq_s[...] = jnp.zeros_like(sq_s)
        mix_s[...] = jnp.zeros_like(mix_s)

    par = par_ref[...]
    summed = conv_silu(sig_ref[...], par, joined)
    conv_ref[...] = summed
    head_in = summed * logistic(summed)
    run_cols = head_columns(run_s[...], step)
    step_cols = head_columns(step_s[...], step)
    runs = [spread(run_cols, head) for head in range(GROUP)]
    steps = [spread(step_cols, head) for head in range(GROUP)]
    tops, bottoms, intos, sources = [], [], [], []
    for pair in range(GROUP // 2):
        lanes = slice(pair * LANES, (pair + 1) * LANES)
        step_size, into, toward = pair_terms(pair, runs, steps)
        scaled = head_in[:, lanes] * step_size
        low = scaled.astype(bf16)
        for block, found in ((0, tops), (1, bottoms)):
            rows = slice(block * BLOCK, (block + 1) * BLOCK)
            first, second = decay_pair(pair, block, runs, runt_s, step)
            mixing = jnp.concatenate([first * score_s[block], second * score_s[block]], axis=1)
            found.append(mm(mixing.astype(bf16), split_heads(low[rows])))
        intos.append(into)
        sources.append((scaled[:BLOCK] * toward).astype(bf16))
    carried = mm(cross_s[...], jnp.concatenate(sources, axis=1)) * jnp.concatenate(intos, axis=1)
    top, bottom = jnp.concatenate(tops, axis=1), jnp.concatenate(bottoms, axis=1)
    heads_ref[:BLOCK] = top
    heads_ref[BLOCK:] = bottom
    heads = jnp.concatenate([top, bottom + carried], axis=0) + par[6:7] * head_in
    gate = gate_ref[...]
    opened = logistic(gate)
    silu = gate * opened
    u = heads * silu
    grad = grad_ref[...]
    mixed = grad * par[5:6] * u
    square = u * u
    sq_s[...] += square[:, :LANES] + square[:, LANES:]
    mix_s[...] += mixed[:, :LANES] + mixed[:, LANES:]
    u_s[step] = u
    silu_s[step] = silu
    slope_s[step] = heads * (opened * (1.0 + gate * (1.0 - opened)))
    grad_s[step] = grad

    @pl.when(step == STEPS - 1)
    def finish():
        scale = lax.rsqrt(jnp.sum(sq_s[...], axis=1, keepdims=True) * (1.0 / INNER) + epsilon)
        rows = scale.shape[0]
        drag = scale * scale * scale * (jnp.sum(mix_s[...], axis=1, keepdims=True) * (1.0 / INNER))
        for part in range(STEPS):
            lanes = slice(part * WIDE, (part + 1) * WIDE)
            gain = gain_ref[:, lanes]
            normal = u_s[part] * scale
            grad = grad_s[part]
            gated = (normal * gain).astype(bf16)
            gated_ref[:, lanes] = gated
            core, place = part // QUARTERS, part % QUARTERS
            sent_ref[place, rows:, core * WIDE : (core + 1) * WIDE] = gated
            gaing_ref[:, lanes] = jnp.sum(grad * normal, axis=0, keepdims=True)
            du = scale * (grad * gain) - u_s[part] * drag
            dheads_ref[:, lanes] = du * silu_s[part]
            dgate = (du * slope_s[part]).astype(bf16)
            dgate_ref[:, lanes] = dgate
            half = part % 2
            sent_ref[part // 2, :rows, half * WIDE : (half + 1) * WIDE] = dgate


def backward_kernel(
    len_ref, raw_ref, head_ref, sig_ref, bc_ref, conv_ref, convbc_ref, dheads_ref, heads_ref, par_ref, parbc_ref,
    dx_ref, dr_ref, late_ref, parg_ref, parbcg_ref, headg_ref,
    joined, step_s, run_s, runt_s, maps_s, score_s, cross_s, dscore_s, dcross_s, dstep_s, ddecay_s,
):
    step = pl.program_id(0)

    @pl.when(step == 0)
    def prepare():
        write_joined(len_ref, joined)
        write_running(raw_ref, head_ref, step_s, run_s, runt_s)
        summed = convbc_ref[...]
        active = summed * logistic(summed)
        maps_s[...] = active
        write_map, read_map = active[:, :NSTATE], active[:, NSTATE:]
        for block in range(2):
            rows = slice(block * BLOCK, (block + 1) * BLOCK)
            scores = mm(read_map[rows], write_map[rows], LANE, highest)
            score_s[block] = jnp.where(linked(len_ref, block * BLOCK, block * BLOCK), scores, 0.0)
        cross = mm(read_map[BLOCK:], write_map[:BLOCK], LANE, highest)
        cross_s[...] = jnp.where(linked(len_ref, BLOCK, 0), cross, 0.0).astype(bf16)
        dscore_s[...] = jnp.zeros_like(dscore_s)
        dcross_s[...] = jnp.zeros_like(dcross_s)
        dstep_s[...] = jnp.zeros_like(dstep_s)
        ddecay_s[...] = jnp.zeros_like(ddecay_s)

    par = par_ref[...]
    summed = conv_ref[...]
    opened = logistic(summed)
    head_in = summed * opened
    slope = opened * (1.0 + summed * (1.0 - opened))
    run_cols = head_columns(run_s[...], step)
    step_cols = head_columns(step_s[...], step)
    runs = [spread(run_cols, head) for head in range(GROUP)]
    steps = [spread(step_cols, head) for head in range(GROUP)]
    dheads = dheads_ref[...]
    dlow = dheads.astype(bf16)
    tops, bottoms, towards, sinks, sources, lows, sizes = [], [], [], [], [], [], []
    for pair in range(GROUP // 2):
        lanes = slice(pair * LANES, (pair + 1) * LANES)
        step_size, into, toward = pair_terms(pair, runs, steps)
        scaled = head_in[:, lanes] * step_size
        low = scaled.astype(bf16)
        for block, found in ((0, tops), (1, bottoms)):
            rows = slice(block * BLOCK, (block + 1) * BLOCK)
            first, second = decay_pair(pair, block, runs, runt_s, step)
            mixing = jnp.concatenate([first * score_s[block], second * score_s[block]], axis=0)
            parted = split_heads(dlow[rows, lanes])
            found.append(mm(mixing.astype(bf16), parted, ROWS))
            dmixing = mm(parted, low[rows], LANE)
            dscore_s[block] += first * dmixing[:BLOCK] + second * dmixing[BLOCK:]
        sinks.append((dheads[BLOCK:, lanes] * into).astype(bf16))
        sources.append((scaled[:BLOCK] * toward).astype(bf16))
        towards.append(toward)
        lows.append(low)
        sizes.append(step_size)
    sink, source = jnp.concatenate(sinks, axis=1), jnp.concatenate(sources, axis=1)
    dcross_s[...] += mm(sink, source, LANE)
    arrived, returned = mm(cross_s[...], source), mm(cross_s[...], sink, ROWS)
    inside = jnp.concatenate([jnp.concatenate(tops, axis=1), jnp.concatenate(bottoms, axis=1)], axis=0)
    dscaled = jnp.concatenate(
        [inside[:BLOCK] + returned * jnp.concatenate(towards, axis=1), inside[BLOCK:]], axis=0
    )
    between = jnp.concatenate([-source.astype(f32) * returned, sink.astype(f32) * arrived], axis=0)
    owner = lax.broadcasted_iota(jnp.int32, (WIDE, LANES), 0) // HEADDIM + GROUP * step
    sums = (owner == lax.broadcasted_iota(jnp.int32, (WIDE, LANES), 1)).astype(f32)
    low = jnp.concatenate(lows, axis=1).astype(f32)
    moved = dlow.astype(f32) * heads_ref[...] - low * inside + between
    ddecay_s[...] += mm(moved, sums, precision=highest)
    dstep_s[...] += mm(head_in * dscaled, sums, precision=highest)
    dhead_in = jnp.concatenate(sizes, axis=1) * dscaled + par[6:7] * dheads

    def store(row, value):
        parg_ref[row : row + 1, :] = value

    store(5, jnp.zeros((1, WIDE), f32))
    store(6, jnp.sum(dheads * head_in, axis=0, keepdims=True))
    store(7, jnp.zeros((1, WIDE), f32))
    dx = conv_back(dhead_in * slope, sig_ref[...], par, joined, store).astype(bf16)
    dx_ref[...] = dx
    late_ref[step // 2, :, pl.ds(pl.multiple_of(lax.rem(step, 2) * WIDE, WIDE), WIDE)] = dx

    @pl.when(step == STEPS - 1)
    def finish():
        maps = maps_s[...]
        write_map, read_map = maps[:, :NSTATE], maps[:, NSTATE:]
        w0, w1, r0, r1 = write_map[:BLOCK], write_map[BLOCK:], read_map[:BLOCK], read_map[BLOCK:]
        d0 = jnp.where(linked(len_ref, 0, 0), dscore_s[0], 0.0)
        d1 = jnp.where(linked(len_ref, BLOCK, BLOCK), dscore_s[1], 0.0)
        dc = jnp.where(linked(len_ref, BLOCK, 0), dcross_s[...], 0.0)
        dread = jnp.concatenate(
            [mm(d0, w0, precision=highest), mm(d1, w1, precision=highest) + mm(dc, w0, precision=highest)], axis=0
        )
        dwrite = jnp.concatenate(
            [mm(d0, r0, ROWS, highest) + mm(dc, r1, ROWS, highest), mm(d1, r1, ROWS, highest)], axis=0
        )
        summed = convbc_ref[...]
        opened = logistic(summed)
        slope = opened * (1.0 + summed * (1.0 - opened))

        def store(row, value):
            parbcg_ref[row : row + 1, :] = value

        for row in (5, 6, 7):
            store(row, jnp.zeros((1, WIDE), f32))
        grad = jnp.concatenate([dwrite, dread], axis=1) * slope
        dmaps = conv_back(grad, bc_ref[...], parbc_ref[...], joined, store).astype(bf16)
        dr_ref[:, :WIDE] = dmaps
        late_ref[0, :, 2 * WIDE :] = dmaps[:, :NSTATE]
        late_ref[1, :, 2 * WIDE :] = dmaps[:, NSTATE:]

        shifted, step_size, rate, decay = step_terms(raw_ref, head_ref)
        change = ddecay_s[...]
        late = mm(lower(), change[BLOCK:], ROWS, highest)
        early = mm(lower(), change[:BLOCK], ROWS, highest) + late[0:1]
        ddecay = jnp.concatenate([early, late], axis=0)
        dshifted = (dstep_s[...] - rate * ddecay) * logistic(shifted)
        lane = lax.broadcasted_iota(jnp.int32, dshifted.shape, 1)
        dshifted = jnp.where(lane < HEADS, dshifted, 0.0)
        dr_ref[:, WIDE:] = dshifted.astype(bf16)
        late_ref[2, :, 2 * WIDE :] = dshifted.astype(bf16)
        late_ref[3, :, 2 * WIDE :] = jnp.zeros_like(dshifted, bf16)
        headg_ref[...] = jnp.zeros_like(headg_ref)
        headg_ref[0:1, :] = jnp.sum(dshifted, axis=0, keepdims=True)
        headg_ref[1:2, :] = jnp.sum(decay * ddecay, axis=0, keepdims=True)


def whole(shape):
    return pl.BlockSpec(shape, lambda step: (0,) * len(shape))


def columns(rows, start=0):
    return pl.BlockSpec((rows, WIDE), lambda step: (0, start + step))


def fixed_columns(rows, start):
    return pl.BlockSpec((rows, WIDE), lambda step: (0, start))


def shape(rows, cols, dtype=f32):
    return jax.ShapeDtypeStruct((rows, cols), dtype)


def params(mebibytes):
    return pltpu.CompilerParams(dimension_semantics=("arbitrary",), vmem_limit_bytes=mebibytes * 1024 * 1024)


def run_forward(lengths, raw, head, projected, gated_grad, par, gain):
    rows = projected.shape[0]
    state = pltpu.VMEM((STEPS, rows, WIDE), f32)
    narrow = pltpu.VMEM((rows, LANES), f32)
    return pl.pallas_call(
        forward_kernel,
        grid=(STEPS,),
        in_specs=[
            pl.BlockSpec(memory_space=pltpu.SMEM),
            whole((rows, LANES)),
            whole((8, LANES)),
            columns(rows, INNER // WIDE),
            fixed_columns(rows, 2 * INNER // WIDE),
            columns(rows),
            columns(rows),
            columns(8),
            fixed_columns(8, INNER // WIDE),
            whole((1, INNER)),
        ],
        out_specs=[
            whole((rows, INNER)), whole((rows, INNER)), whole((QUARTERS, 2 * rows, 2 * WIDE)), whole((rows, INNER)),
            columns(rows), columns(rows), whole((rows, WIDE)), whole((1, INNER)),
        ],
        out_shape=[
            shape(rows, INNER, bf16), shape(rows, INNER, bf16),
            jax.ShapeDtypeStruct((QUARTERS, 2 * rows, 2 * WIDE), bf16), shape(rows, INNER),
            shape(rows, INNER), shape(rows, INNER), shape(rows, WIDE), shape(1, INNER),
        ],
        scratch_shapes=[
            pltpu.VMEM((CONV_WIDTH - 1, rows, LANES), f32),
            narrow, narrow, pltpu.VMEM((STEPS, 8, rows), f32),
            pltpu.VMEM((2, BLOCK, BLOCK), f32), pltpu.VMEM((BLOCK, BLOCK), bf16),
            state, state, state, state, narrow, narrow,
        ],
        compiler_params=params(28),
        cost_estimate=pl.CostEstimate(flops=15_000_000_000, bytes_accessed=16_000_000, transcendentals=3_000_000),
        name="mixer_forward",
    )(lengths, raw, head, projected, projected, projected, gated_grad, par, par, gain)


def run_backward(lengths, raw, head, projected, conv, convbc, dheads, heads, par):
    rows = projected.shape[0]
    narrow = pltpu.VMEM((rows, LANES), f32)
    square = pltpu.VMEM((2, BLOCK, BLOCK), f32)
    return pl.pallas_call(
        backward_kernel,
        grid=(STEPS,),
        in_specs=[
            pl.BlockSpec(memory_space=pltpu.SMEM),
            whole((rows, LANES)),
            whole((8, LANES)),
            columns(rows, INNER // WIDE),
            fixed_columns(rows, 2 * INNER // WIDE),
            columns(rows), whole((rows, WIDE)), columns(rows), columns(rows),
            columns(8),
            fixed_columns(8, INNER // WIDE),
        ],
        out_specs=[
            columns(rows), whole((rows, WIDE + LANES)), whole((QUARTERS, rows, LATE)), columns(8), whole((8, WIDE)), whole((8, LANES)),
        ],
        out_shape=[
            shape(rows, INNER, bf16), shape(rows, WIDE + LANES, bf16),
            jax.ShapeDtypeStruct((QUARTERS, rows, LATE), bf16), shape(8, INNER), shape(8, WIDE), shape(8, LANES),
        ],
        scratch_shapes=[
            pltpu.VMEM((CONV_WIDTH - 1, rows, LANES), f32),
            narrow, narrow, pltpu.VMEM((STEPS, 8, rows), f32), pltpu.VMEM((rows, WIDE), f32),
            square, pltpu.VMEM((BLOCK, BLOCK), bf16), square, pltpu.VMEM((BLOCK, BLOCK), f32), narrow, narrow,
        ],
        compiler_params=params(20),
        cost_estimate=pl.CostEstimate(flops=20_000_000_000, bytes_accessed=16_000_000, transcendentals=3_000_000),
        name="mixer_backward",
    )(lengths, raw, head, projected, projected, conv, convbc, dheads, heads, par, par)


def normalized(value, gain):
    scale = lax.rsqrt(jnp.mean(value * value, axis=-1, keepdims=True) + epsilon)
    return scale, (value * scale * gain).astype(bf16)


def known_kernel(core_ref, gain_ref, first, second, third, fourth, mine_ref, theirs_ref, up_ref):
    half = mine_ref.shape[1]
    for at, ref in enumerate((first, second, third, fourth)):
        count = ref.shape[0] // 2
        rows = slice(at * count, (at + 1) * count)
        unused, normed = normalized(ref[:count].astype(f32), gain_ref[...])
        low, high = normed[:, :half], normed[:, half:]
        is_first = core_ref[0] == 0
        mine_ref[rows] = jnp.where(is_first, low, high)
        theirs_ref[rows] = jnp.where(is_first, high, low)
        up_ref[rows] = ref[count:]


def run_known(core, gain, known):
    count, model = known[0].shape[0] // 2, known[0].shape[1]
    every = QUARTERS * count
    return pl.pallas_call(
        known_kernel,
        in_specs=[pl.BlockSpec(memory_space=pltpu.SMEM)] + [pl.BlockSpec(memory_space=pltpu.VMEM)] * 5,
        out_specs=[pl.BlockSpec(memory_space=pltpu.VMEM)] * 3,
        out_shape=[shape(every, model // 2, bf16), shape(every, model // 2, bf16), shape(every, model, bf16)],
        compiler_params=pltpu.CompilerParams(vmem_limit_bytes=32 * 1024 * 1024),
        cost_estimate=pl.CostEstimate(flops=1, bytes_accessed=1, transcendentals=0),
        name="known_rows",
    )(core, gain, *known)


def early_kernel(core_ref, first, second, third, fourth, send_ref, own_ref):
    gate = 2 * WIDE
    for at, ref in enumerate((first, second, third, fourth)):
        count = ref.shape[0] // 2
        rows = slice(at * count, (at + 1) * count)
        low, high = ref[count:, :WIDE], ref[count:, WIDE:]
        is_first = core_ref[0] == 0
        send_ref[rows, :gate] = ref[:count]
        send_ref[rows, gate:] = jnp.where(is_first, high, low)
        own_ref[rows] = jnp.where(is_first, low, high)


def run_early(core, got):
    every = QUARTERS * got[0].shape[0] // 2
    return pl.pallas_call(
        early_kernel,
        in_specs=[pl.BlockSpec(memory_space=pltpu.SMEM)] + [pl.BlockSpec(memory_space=pltpu.VMEM)] * 4,
        out_specs=[pl.BlockSpec(memory_space=pltpu.VMEM)] * 2,
        out_shape=[shape(every, 3 * WIDE, bf16), shape(every, WIDE, bf16)],
        compiler_params=pltpu.CompilerParams(vmem_limit_bytes=32 * 1024 * 1024),
        cost_estimate=pl.CostEstimate(flops=1, bytes_accessed=1, transcendentals=0),
        name="early_factors",
    )(core, *got)


def finish_kernel(side_ref, base_ref, first, first_got, second, second_got, out_ref, rows_s, sems):
    half = first.shape[0] // 2
    body, wide_cols = half - NSTATE, 2 * WIDE
    sizes = [wide_cols] * QUARTERS + [rows_s.shape[0] - INNER]
    moves = [
        pltpu.make_async_copy(
            rows_s.at[pl.ds(at * wide_cols, size)], out_ref.at[pl.ds(INNER + at * wide_cols, size)], sems.at[at]
        )
        for at, size in enumerate(sizes)
    ]
    for place in range(QUARTERS):
        x, y = place // 2, place % 2
        top = slice(y * half, (y + 1) * half)
        start = place * wide_cols
        rows_s[start : start + half] = jnp.where(side_ref[0] == x, first[top], first_got[top]).astype(f32)
        low = slice(x * half, (x + 1) * half)
        value = jnp.where(side_ref[1] == y, second[low], second_got[low]).astype(f32)
        rows_s[start + half : start + wide_cols] = value[:body]
        keep = min(NSTATE, max(0, rows_s.shape[0] - INNER - place * NSTATE))
        if keep:
            rows_s[INNER + place * NSTATE : INNER + place * NSTATE + keep] = value[body : body + keep]
        moves[place].start()
    moves[QUARTERS].start()
    for move in moves:
        move.wait()


def run_finish(sides, base, first, first_got, second, second_got):
    late_rows = base.shape[0] - INNER
    return pl.pallas_call(
        finish_kernel,
        in_specs=[pl.BlockSpec(memory_space=pltpu.SMEM), pl.BlockSpec(memory_space=pl.ANY)]
        + [pl.BlockSpec(memory_space=pltpu.VMEM)] * 4,
        out_specs=pl.BlockSpec(memory_space=pl.ANY),
        out_shape=jax.ShapeDtypeStruct(base.shape, f32),
        scratch_shapes=[pltpu.VMEM((late_rows, base.shape[1]), f32), pltpu.SemaphoreType.DMA((QUARTERS + 1,))],
        input_output_aliases={1: 0},
        compiler_params=pltpu.CompilerParams(vmem_limit_bytes=24 * 1024 * 1024),
        cost_estimate=pl.CostEstimate(flops=1, bytes_accessed=8_000_000, transcendentals=0),
        name="late_rows",
    )(sides, base, first, first_got, second, second_got)


def make_shards(mesh):
    reps = mesh.shape["rep"]
    bits = reps.bit_length() - 1
    assert reps == 1 << bits and bits >= 2 and mesh.shape["shard"] == 2
    up_order, down_order = tuple(range(2, bits)), tuple(reversed(range(2, bits)))
    far = len(up_order)

    def swap(value):
        return lax.ppermute(value, "shard", [(0, 1), (1, 0)])

    def across(value, flip):
        return lax.ppermute(value, "rep", [(place, place ^ flip) for place in range(reps)])

    def side_of(bit):
        return (lax.axis_index("rep") >> bit) & 1

    def quarter_of(flip):
        place = lax.axis_index("rep") ^ flip
        return (place & 1) * 2 + ((place >> 1) & 1)

    def joined(side, mine, theirs, axis):
        return jnp.where(
            side == 0, jnp.concatenate([mine, theirs], axis=axis), jnp.concatenate([theirs, mine], axis=axis)
        )

    def part(value, bit, flip):
        half = value.shape[0] // 2
        return lax.dynamic_slice_in_dim(value, (side_of(bit) ^ flip) * half, half)

    def terms(smalls):
        high = lax.reduce_precision(smalls, 8, 7)
        return jnp.concatenate([high.astype(bf16), (smalls - high).astype(bf16)], axis=0)

    def exchange(value, bit, smalls):
        if smalls is None:
            return across(value, 1 << bit), None
        rows, count = value.shape[0], smalls.shape[0]
        got = across(jnp.concatenate([value, terms(smalls)], axis=0), 1 << bit)
        added = got[rows:].astype(f32)
        return got[:rows], smalls + added[:count] + added[count:]

    def scatter(value, bit, smalls=None):
        got, smalls = exchange(part(value, bit, 1).astype(bf16), bit, smalls)
        return part(value, bit, 0) + got.astype(f32), smalls

    def gather(value, bit, smalls=None):
        got, smalls = exchange(value, bit, smalls)
        return joined(side_of(bit), value, got, 0), smalls

    def pair_step(pieces, at, smalls=None, carrier=1):
        beside = [None, None]
        beside[carrier] = smalls
        moved = []
        for which, value in enumerate(pieces):
            order = (up_order, down_order)[which]
            if at < far:
                moved.append(scatter(value, order[at], beside[which]))
            else:
                value = value.astype(bf16) if at == far else value
                late_at = at - 2 * far
                bit = order[2 * far - 1 - at] if late_at < 0 else (1 - late_at, late_at)[which]
                moved.append(gather(value, bit, beside[which]))
        return tuple(value for value, _ in moved), moved[carrier][1]

    steps = 2 * far + 2

    def turned(value):
        size = value.shape[0] // QUARTERS
        return [value[at * size : (at + 1) * size] for at in (0, 2, 1, 3)]

    def shards(
        tokens, lengths, norm_gain, in_weight, conv_weight, conv_bias, step_bias, decay_log, skip_gain,
        gate_gain, out_weight, cotangent,
    ):
        core = lax.axis_index("shard")
        rows, model = tokens.shape
        half_model, half_inner = model // 2, INNER // 2
        half_conv, half_heads = CONVDIM // 2, HEADS // 2

        def mine(value, size):
            return lax.dynamic_slice_in_dim(value, core * size, size, axis=1)

        def theirs(value, size):
            return lax.dynamic_slice_in_dim(value, (1 - core) * size, size, axis=1)

        live = (jnp.arange(rows, dtype=jnp.int32) < jnp.sum(lengths))[:, None]
        upstream = jnp.where(live, cotangent, jnp.zeros_like(cotangent))
        known = jnp.concatenate([tokens, upstream], axis=0)
        known = [known, *(across(known, flip) for flip in (1, 2, 3))]

        def line(value):
            return jnp.pad(value, (0, half_conv - value.shape[0]))[None]

        small = jnp.concatenate(
            [
                conv_weight.T, conv_bias[None], line(gate_gain),
                line(jnp.concatenate([norm_gain, step_bias, decay_log, skip_gain])),
                jnp.zeros((1, half_conv), bf16),
            ],
            axis=0,
        )
        small_o = swap(small)
        in_other = swap(in_weight)
        out_other = swap(out_weight)
        small, small_o = small.astype(f32), small_o.astype(f32)
        low_half, high_half = jnp.where(core == 0, small, small_o), jnp.where(core == 0, small_o, small)
        both = jnp.concatenate([low_half, high_half], axis=1)

        def pick(row, start, size):
            return jnp.concatenate([low_half[row, start : start + size], high_half[row, start : start + size]])

        norm_scale = pick(6, 0, half_model)
        head_lines = [pick(6, half_model + at * half_heads, half_heads) for at in range(3)]
        gate_line = pick(5, 0, half_inner)[None]
        par = jnp.concatenate(
            [
                both[:5],
                jnp.pad(gate_line, ((0, 0), (0, CONVDIM - INNER))),
                jnp.pad(jnp.repeat(head_lines[2], HEADDIM)[None], ((0, 0), (0, CONVDIM - INNER))),
                jnp.zeros((1, CONVDIM), f32),
            ],
            axis=0,
        )
        head = jnp.pad(jnp.stack(head_lines[:2]), ((0, 6), (0, LANES - HEADS)))

        inputs = tokens.astype(f32)
        scale, normed = normalized(inputs, norm_scale)
        normed_m, normed_o = mine(normed, half_model), theirs(normed, half_model)

        gated_grad = joined(core, mm(upstream, out_weight, LANE), mm(upstream, out_other, LANE), 1)
        projected = mm(normed_m, in_weight) + mm(normed_o, in_other)
        raw = jnp.pad(projected[:, STEP_COL:], ((0, 0), (0, LANES - HEADS)))
        gated, dgate, leaving, dheads, heads, conv, convbc, gain_g = run_forward(
            lengths, raw, head, projected, gated_grad, par, gate_line
        )

        def quarters(value):
            return [lax.dynamic_index_in_dim(value, quarter_of(flip), 0, keepdims=False) for flip in range(QUARTERS)]

        early_sent = quarters(leaving)
        early_got = [early_sent[0], *(across(early_sent[flip], flip) for flip in (1, 2, 3))]
        dx, dr, late, par_g, parbc_g, head_g = run_backward(
            lengths, raw, head, projected, conv, convbc, dheads, heads, par
        )

        late_sent = quarters(late)
        late_sent, known = lax.optimization_barrier((late_sent, known))
        place = core.astype(jnp.int32)[None]
        known_m, known_t, known_up = run_known(place, norm_scale[None], known)
        known_o, known_up_o = swap(known_t), swap(known_up)
        late_got = [late_sent[0], *(across(late_sent[flip], flip) for flip in (1, 2, 3))]
        early_m, early_out_m = run_early(place, early_got)
        early_o = swap(early_m)
        gate_cols = 2 * WIDE
        early = (
            mm(early_out_m, known_up, ROWS) + mm(early_o[:, gate_cols:], known_up_o, ROWS),
            mm(early_m[:, :gate_cols], known_m, ROWS) + mm(early_o[:, :gate_cols], known_o, ROWS),
        )
        early, gated, late_got = lax.optimization_barrier((early, gated, late_got))
        early, _ = pair_step(early, 0)
        gated_m, gated_o = mine(gated, half_inner), theirs(gated, half_inner)
        branch = mm(gated_m, out_weight) + mm(gated_o, out_other)
        output = (inputs + jnp.where(live, branch, 0.0)).astype(bf16)
        late_all = jnp.concatenate(late_got, axis=0)
        late_all_o = swap(late_all)

        early, dx, dr, dgate, late_all, output = lax.optimization_barrier((early, dx, dr, dgate, late_all, output))
        early, _ = pair_step(early, 1)
        late_grad = mm(late_all, known_m, ROWS) + mm(late_all_o, known_o, ROWS)
        late_tail = dr[:, : CONVDIM - INNER + HEADS]
        proj_grad = jnp.concatenate([dgate, dx, late_tail], axis=1)
        early, late_grad, proj_grad = lax.optimization_barrier((early, late_grad, proj_grad))
        early, _ = pair_step(early, 2)
        normed_grad_m = mm(proj_grad, in_weight, LANE)
        early, normed_grad_m, proj_grad = lax.optimization_barrier((early, normed_grad_m, proj_grad))
        early, _ = pair_step(early, 3)
        normed_grad = joined(core, normed_grad_m, mm(proj_grad, in_other, LANE), 1)
        g = normed_grad * norm_scale
        input_grad = (
            cotangent.astype(f32)
            + scale * g
            - inputs * (scale * scale * scale * jnp.mean(g * inputs, axis=-1, keepdims=True))
        )
        gain_grad = jnp.sum(normed_grad * inputs * scale, axis=0)

        skip_g = jnp.sum(par_g[6].reshape(HEADS, HEADDIM), axis=1)
        tail = jnp.concatenate([gain_grad, head_g[0, :HEADS], head_g[1, :HEADS], skip_g])
        total = jnp.concatenate(
            [
                jnp.concatenate([par_g[:5], parbc_g[:5]], axis=1),
                jnp.pad(gain_g, ((0, 0), (0, CONVDIM - INNER))),
                jnp.pad(tail, (0, CONVDIM - tail.shape[0]))[None],
                jnp.zeros((1, CONVDIM), f32),
            ],
            axis=0,
        )
        smalls = (total + swap(total)).reshape(-1, half_model)
        early, late_grad, input_grad, smalls = lax.optimization_barrier((early, late_grad, input_grad, smalls))
        half_late = LATE // 2
        late_parts = (late_grad[:half_late], late_grad[half_late:])
        last = 2 * far + 1
        last = 2 * far + 1
        for at in range(4, steps):
            early, smalls = pair_step(early, at, smalls) if at == last - 1 else (pair_step(early, at)[0], smalls)
            for late_at in {last - 1: range(1), last: range(1, 2 * far)}.get(at, ()):
                if 1 <= late_at < far or late_at == 2 * far - 1:
                    late_parts, smalls = pair_step(late_parts, late_at, smalls)
                else:
                    late_parts, _ = pair_step(late_parts, late_at)
            if at >= last - 1:
                early, late_parts = lax.optimization_barrier((early, late_parts))
        late_parts, smalls = pair_step(late_parts, steps - 2, smalls, 0)
        out_grad = early[0].astype(f32)
        late_parts, out_grad = lax.optimization_barrier((late_parts, out_grad))
        in_grad = jnp.concatenate(
            [*turned(early[1]), jnp.zeros((STEP_COL + HEADS - INNER, half_model), bf16)], axis=0
        ).astype(f32)
        total = smalls.reshape(total.shape)

        def own(row, start, size):
            return lax.dynamic_slice_in_dim(total[row], start + core * size, size)

        small_grads = (
            own(6, 0, half_model),
            lax.dynamic_slice_in_dim(total[:4], core * half_conv, half_conv, axis=1).T,
            own(4, 0, half_conv),
            own(6, model, half_heads),
            own(6, model + HEADS, half_heads),
            own(6, model + 2 * HEADS, half_heads),
            own(5, 0, half_inner),
        )
        in_grad, small_grads = lax.optimization_barrier((in_grad, small_grads))
        sides = jnp.stack([side_of(0), side_of(1)]).astype(jnp.int32)
        in_grad = run_finish(
            sides, in_grad, late_parts[0], across(late_parts[0], 1), late_parts[1], across(late_parts[1], 2)
        ).T
        norm_grad, conv_grad, bias_grad, step_grad, decay_grad, skip_grad, gate_grad = small_grads

        return (
            output, input_grad, norm_grad, in_grad, conv_grad, bias_grad, step_grad, decay_grad, skip_grad,
            gate_grad, out_grad,
        )

    return shards


def solution(mesh):
    split = P(("rep", "shard"), None)
    vector, matrix = P("shard"), P("shard", None)
    in_specs = (
        split, split, vector, matrix, matrix, vector, vector, vector, vector, vector, matrix, split,
    )
    out_specs = (
        split, split, vector, matrix, matrix, vector, vector, vector, vector, vector, matrix,
    )
    return jax.shard_map(make_shards(mesh), mesh=mesh, in_specs=in_specs, out_specs=out_specs, check_vma=False)
```

```python
import jax
import jax.numpy as jnp
from jax import lax
from jax.experimental import pallas as pl
from jax.experimental.pallas import tpu as pltpu
from jax.sharding import PartitionSpec as P

HEADS = 32
HEADDIM = 64
NSTATE = 128
CONV_WIDTH = 4
BLOCK = 128
INNER = 2048
CONVDIM = 2304
STEP_COL = INNER + CONVDIM

GROUP = 4
WIDE = GROUP * HEADDIM
STEPS = HEADS // GROUP
QUARTERS = 4
LATE = INNER // QUARTERS + NSTATE
LANES = 128

epsilon = 1e-05
highest = lax.Precision.HIGHEST
f32 = jnp.float32
bf16 = jnp.bfloat16


def mm(left, right, dims=((1,), (0,)), precision=None):
    return lax.dot_general(left, right, (dims, ((), ())), precision=precision, preferred_element_type=f32)


LANE = ((1,), (1,))
ROWS = ((0,), (0,))


def segment_of(places, len_ref):
    end = len_ref[0, 0]
    segment = (places >= end).astype(jnp.int32)
    for slot in range(1, len_ref.shape[1]):
        end = end + len_ref[0, slot]
        segment = segment + (places >= end).astype(jnp.int32)
    return segment


def write_joined(len_ref, joined_ref):
    rows, lanes = joined_ref.shape[1:]
    places = lax.broadcasted_iota(jnp.int32, (rows, lanes), 0)
    segment = segment_of(places, len_ref)
    for offset in range(1, CONV_WIDTH):
        same = (segment_of(places - offset, len_ref) == segment) & (places >= offset)
        joined_ref[offset - 1] = same.astype(f32)


def wide(mask):
    return jnp.concatenate([mask, mask], axis=1)


def linked(len_ref, row_start, col_start):
    rows = lax.broadcasted_iota(jnp.int32, (BLOCK, BLOCK), 0) + row_start
    cols = lax.broadcasted_iota(jnp.int32, (BLOCK, BLOCK), 1) + col_start
    return (segment_of(rows, len_ref) == segment_of(cols, len_ref)) & (rows >= cols)


def step_terms(raw_ref, head_ref):
    lane = lax.broadcasted_iota(jnp.int32, raw_ref.shape, 1)
    shifted = jnp.where(lane < HEADS, raw_ref[...] + head_ref[0:1, :], 0.0)
    step = jnp.maximum(shifted, 0.0) + jnp.log1p(jnp.exp(-jnp.abs(shifted)))
    rate = jnp.exp(head_ref[1:2, :])
    return shifted, step, rate, -step * rate


def lower():
    rows = lax.broadcasted_iota(jnp.int32, (BLOCK, BLOCK), 0)
    cols = lax.broadcasted_iota(jnp.int32, (BLOCK, BLOCK), 1)
    return (rows >= cols).astype(f32)


def write_running(raw_ref, head_ref, step_ref, run_ref, runt_ref):
    unused, step, rate, decay = step_terms(raw_ref, head_ref)
    step_ref[...] = step
    for block in range(2):
        rows = slice(block * BLOCK, (block + 1) * BLOCK)
        running = mm(lower(), decay[rows], precision=highest)
        run_ref[rows, :] = running
        turned = running.T
        for group in range(STEPS):
            runt_ref[group, 0:GROUP, rows] = turned[group * GROUP : (group + 1) * GROUP]


def conv_silu(signal, par, joined_ref):
    summed = par[4:5] + signal * par[3:4]
    for offset in range(1, CONV_WIDTH):
        tap = par[3 - offset : 4 - offset]
        summed = summed + pltpu.roll(signal, offset, 0) * wide(joined_ref[offset - 1]) * tap
    return summed


def conv_back(grad, signal, par, joined_ref, store):
    rows = grad.shape[0]
    back = grad * par[3:4]
    store(3, jnp.sum(grad * signal, axis=0, keepdims=True))
    store(4, jnp.sum(grad, axis=0, keepdims=True))
    for offset in range(1, CONV_WIDTH):
        masked = grad * wide(joined_ref[offset - 1])
        store(3 - offset, jnp.sum(masked * pltpu.roll(signal, offset, 0), axis=0, keepdims=True))
        back = back + pltpu.roll(masked, rows - offset, 0) * par[3 - offset : 4 - offset]
    return back


def logistic(value):
    return 0.5 * jnp.tanh(0.5 * value) + 0.5


def head_columns(table, step):
    return pltpu.roll(table, lax.rem(LANES - GROUP * step, LANES), 1)


def spread(columns, head):
    return jnp.broadcast_to(columns[:, head : head + 1], (columns.shape[0], LANES))


def half_lanes(shape):
    return lax.broadcasted_iota(jnp.int32, shape, 1) < HEADDIM


def decay_pair(pair, block, runs, runt_ref, step):
    rows = slice(block * BLOCK, (block + 1) * BLOCK)
    out = []
    for place in (2 * pair, 2 * pair + 1):
        row = runt_ref[step, place : place + 1, rows]
        out.append(jnp.exp(jnp.minimum(runs[place][rows] - row, 0.0)))
    return out


def split_heads(value):
    first = half_lanes(value.shape)
    zero = jnp.zeros_like(value)
    return jnp.concatenate([jnp.where(first, value, zero), jnp.where(first, zero, value)], axis=0)


def pair_terms(pair, runs, steps):
    first = half_lanes(runs[0].shape)
    run = jnp.where(first, runs[2 * pair], runs[2 * pair + 1])
    step = jnp.where(first, steps[2 * pair], steps[2 * pair + 1])
    into = jnp.exp(run[BLOCK:])
    toward = jnp.exp(run[BLOCK - 1 : BLOCK] - run[:BLOCK])
    return step, into, toward


def forward_kernel(
    len_ref, raw_ref, head_ref, sig_ref, bc_ref, gate_ref, grad_ref, par_ref, parbc_ref, gain_ref,
    gated_ref, dgate_ref, sent_ref, dheads_ref, heads_ref, conv_ref, convbc_ref, gaing_ref,
    joined, step_s, run_s, runt_s, score_s, cross_s, u_s, silu_s, slope_s, grad_s, sq_s, mix_s,
):
    step = pl.program_id(0)

    @pl.when(step == 0)
    def prepare():
        write_joined(len_ref, joined)
        write_running(raw_ref, head_ref, step_s, run_s, runt_s)
        summed = conv_silu(bc_ref[...], parbc_ref[...], joined)
        convbc_ref[...] = summed
        active = summed * logistic(summed)
        write_map, read_map = active[:, :NSTATE], active[:, NSTATE:]
        for block in range(2):
            rows = slice(block * BLOCK, (block + 1) * BLOCK)
            scores = mm(read_map[rows], write_map[rows], LANE, highest)
            score_s[block] = jnp.where(linked(len_ref, block * BLOCK, block * BLOCK), scores, 0.0)
        cross = mm(read_map[BLOCK:], write_map[:BLOCK], LANE, highest)
        cross_s[...] = jnp.where(linked(len_ref, BLOCK, 0), cross, 0.0).astype(bf16)
        sq_s[...] = jnp.zeros_like(sq_s)
        mix_s[...] = jnp.zeros_like(mix_s)

    par = par_ref[...]
    summed = conv_silu(sig_ref[...], par, joined)
    conv_ref[...] = summed
    head_in = summed * logistic(summed)
    run_cols = head_columns(run_s[...], step)
    step_cols = head_columns(step_s[...], step)
    runs = [spread(run_cols, head) for head in range(GROUP)]
    steps = [spread(step_cols, head) for head in range(GROUP)]
    tops, bottoms, intos, sources = [], [], [], []
    for pair in range(GROUP // 2):
        lanes = slice(pair * LANES, (pair + 1) * LANES)
        step_size, into, toward = pair_terms(pair, runs, steps)
        scaled = head_in[:, lanes] * step_size
        low = scaled.astype(bf16)
        for block, found in ((0, tops), (1, bottoms)):
            rows = slice(block * BLOCK, (block + 1) * BLOCK)
            first, second = decay_pair(pair, block, runs, runt_s, step)
            mixing = jnp.concatenate([first * score_s[block], second * score_s[block]], axis=1)
            found.append(mm(mixing.astype(bf16), split_heads(low[rows])))
        intos.append(into)
        sources.append((scaled[:BLOCK] * toward).astype(bf16))
    carried = mm(cross_s[...], jnp.concatenate(sources, axis=1)) * jnp.concatenate(intos, axis=1)
    top, bottom = jnp.concatenate(tops, axis=1), jnp.concatenate(bottoms, axis=1)
    heads_ref[:BLOCK] = top
    heads_ref[BLOCK:] = bottom
    heads = jnp.concatenate([top, bottom + carried], axis=0) + par[6:7] * head_in
    gate = gate_ref[...]
    opened = logistic(gate)
    silu = gate * opened
    u = heads * silu
    grad = grad_ref[...]
    mixed = grad * par[5:6] * u
    square = u * u
    sq_s[...] += square[:, :LANES] + square[:, LANES:]
    mix_s[...] += mixed[:, :LANES] + mixed[:, LANES:]
    u_s[step] = u
    silu_s[step] = silu
    slope_s[step] = heads * (opened * (1.0 + gate * (1.0 - opened)))
    grad_s[step] = grad

    @pl.when(step == STEPS - 1)
    def finish():
        scale = lax.rsqrt(jnp.sum(sq_s[...], axis=1, keepdims=True) * (1.0 / INNER) + epsilon)
        rows = scale.shape[0]
        drag = scale * scale * scale * (jnp.sum(mix_s[...], axis=1, keepdims=True) * (1.0 / INNER))
        for part in range(STEPS):
            lanes = slice(part * WIDE, (part + 1) * WIDE)
            gain = gain_ref[:, lanes]
            normal = u_s[part] * scale
            grad = grad_s[part]
            gated = (normal * gain).astype(bf16)
            gated_ref[:, lanes] = gated
            core, place = part // QUARTERS, part % QUARTERS
            sent_ref[place, rows:, core * WIDE : (core + 1) * WIDE] = gated
            gaing_ref[:, lanes] = jnp.sum(grad * normal, axis=0, keepdims=True)
            du = scale * (grad * gain) - u_s[part] * drag
            dheads_ref[:, lanes] = du * silu_s[part]
            dgate = (du * slope_s[part]).astype(bf16)
            dgate_ref[:, lanes] = dgate
            half = part % 2
            sent_ref[part // 2, :rows, half * WIDE : (half + 1) * WIDE] = dgate


def backward_kernel(
    len_ref, raw_ref, head_ref, sig_ref, bc_ref, conv_ref, convbc_ref, dheads_ref, heads_ref, par_ref, parbc_ref,
    dx_ref, dr_ref, late_ref, parg_ref, parbcg_ref, headg_ref,
    joined, step_s, run_s, runt_s, maps_s, score_s, cross_s, dscore_s, dcross_s, dstep_s, ddecay_s,
):
    step = pl.program_id(0)

    @pl.when(step == 0)
    def prepare():
        write_joined(len_ref, joined)
        write_running(raw_ref, head_ref, step_s, run_s, runt_s)
        summed = convbc_ref[...]
        active = summed * logistic(summed)
        maps_s[...] = active
        write_map, read_map = active[:, :NSTATE], active[:, NSTATE:]
        for block in range(2):
            rows = slice(block * BLOCK, (block + 1) * BLOCK)
            scores = mm(read_map[rows], write_map[rows], LANE, highest)
            score_s[block] = jnp.where(linked(len_ref, block * BLOCK, block * BLOCK), scores, 0.0)
        cross = mm(read_map[BLOCK:], write_map[:BLOCK], LANE, highest)
        cross_s[...] = jnp.where(linked(len_ref, BLOCK, 0), cross, 0.0).astype(bf16)
        dscore_s[...] = jnp.zeros_like(dscore_s)
        dcross_s[...] = jnp.zeros_like(dcross_s)
        dstep_s[...] = jnp.zeros_like(dstep_s)
        ddecay_s[...] = jnp.zeros_like(ddecay_s)

    par = par_ref[...]
    summed = conv_ref[...]
    opened = logistic(summed)
    head_in = summed * opened
    slope = opened * (1.0 + summed * (1.0 - opened))
    run_cols = head_columns(run_s[...], step)
    step_cols = head_columns(step_s[...], step)
    runs = [spread(run_cols, head) for head in range(GROUP)]
    steps = [spread(step_cols, head) for head in range(GROUP)]
    dheads = dheads_ref[...]
    dlow = dheads.astype(bf16)
    tops, bottoms, towards, sinks, sources, lows, sizes = [], [], [], [], [], [], []
    for pair in range(GROUP // 2):
        lanes = slice(pair * LANES, (pair + 1) * LANES)
        step_size, into, toward = pair_terms(pair, runs, steps)
        scaled = head_in[:, lanes] * step_size
        low = scaled.astype(bf16)
        for block, found in ((0, tops), (1, bottoms)):
            rows = slice(block * BLOCK, (block + 1) * BLOCK)
            first, second = decay_pair(pair, block, runs, runt_s, step)
            mixing = jnp.concatenate([first * score_s[block], second * score_s[block]], axis=0)
            parted = split_heads(dlow[rows, lanes])
            found.append(mm(mixing.astype(bf16), parted, ROWS))
            dmixing = mm(parted, low[rows], LANE)
            dscore_s[block] += first * dmixing[:BLOCK] + second * dmixing[BLOCK:]
        sinks.append((dheads[BLOCK:, lanes] * into).astype(bf16))
        sources.append((scaled[:BLOCK] * toward).astype(bf16))
        towards.append(toward)
        lows.append(low)
        sizes.append(step_size)
    sink, source = jnp.concatenate(sinks, axis=1), jnp.concatenate(sources, axis=1)
    dcross_s[...] += mm(sink, source, LANE)
    arrived, returned = mm(cross_s[...], source), mm(cross_s[...], sink, ROWS)
    inside = jnp.concatenate([jnp.concatenate(tops, axis=1), jnp.concatenate(bottoms, axis=1)], axis=0)
    dscaled = jnp.concatenate(
        [inside[:BLOCK] + returned * jnp.concatenate(towards, axis=1), inside[BLOCK:]], axis=0
    )
    between = jnp.concatenate([-source.astype(f32) * returned, sink.astype(f32) * arrived], axis=0)
    owner = lax.broadcasted_iota(jnp.int32, (WIDE, LANES), 0) // HEADDIM + GROUP * step
    sums = (owner == lax.broadcasted_iota(jnp.int32, (WIDE, LANES), 1)).astype(f32)
    low = jnp.concatenate(lows, axis=1).astype(f32)
    moved = dlow.astype(f32) * heads_ref[...] - low * inside + between
    ddecay_s[...] += mm(moved, sums, precision=highest)
    dstep_s[...] += mm(head_in * dscaled, sums, precision=highest)
    dhead_in = jnp.concatenate(sizes, axis=1) * dscaled + par[6:7] * dheads

    def store(row, value):
        parg_ref[row : row + 1, :] = value

    store(5, jnp.zeros((1, WIDE), f32))
    store(6, jnp.sum(dheads * head_in, axis=0, keepdims=True))
    store(7, jnp.zeros((1, WIDE), f32))
    dx = conv_back(dhead_in * slope, sig_ref[...], par, joined, store).astype(bf16)
    dx_ref[...] = dx
    late_ref[step // 2, :, pl.ds(pl.multiple_of(lax.rem(step, 2) * WIDE, WIDE), WIDE)] = dx

    @pl.when(step == STEPS - 1)
    def finish():
        maps = maps_s[...]
        write_map, read_map = maps[:, :NSTATE], maps[:, NSTATE:]
        w0, w1, r0, r1 = write_map[:BLOCK], write_map[BLOCK:], read_map[:BLOCK], read_map[BLOCK:]
        d0 = jnp.where(linked(len_ref, 0, 0), dscore_s[0], 0.0)
        d1 = jnp.where(linked(len_ref, BLOCK, BLOCK), dscore_s[1], 0.0)
        dc = jnp.where(linked(len_ref, BLOCK, 0), dcross_s[...], 0.0)
        dread = jnp.concatenate(
            [mm(d0, w0, precision=highest), mm(d1, w1, precision=highest) + mm(dc, w0, precision=highest)], axis=0
        )
        dwrite = jnp.concatenate(
            [mm(d0, r0, ROWS, highest) + mm(dc, r1, ROWS, highest), mm(d1, r1, ROWS, highest)], axis=0
        )
        summed = convbc_ref[...]
        opened = logistic(summed)
        slope = opened * (1.0 + summed * (1.0 - opened))

        def store(row, value):
            parbcg_ref[row : row + 1, :] = value

        for row in (5, 6, 7):
            store(row, jnp.zeros((1, WIDE), f32))
        grad = jnp.concatenate([dwrite, dread], axis=1) * slope
        dmaps = conv_back(grad, bc_ref[...], parbc_ref[...], joined, store).astype(bf16)
        dr_ref[:, :WIDE] = dmaps
        late_ref[0, :, 2 * WIDE :] = dmaps[:, :NSTATE]
        late_ref[1, :, 2 * WIDE :] = dmaps[:, NSTATE:]

        shifted, step_size, rate, decay = step_terms(raw_ref, head_ref)
        change = ddecay_s[...]
        late = mm(lower(), change[BLOCK:], ROWS, highest)
        early = mm(lower(), change[:BLOCK], ROWS, highest) + late[0:1]
        ddecay = jnp.concatenate([early, late], axis=0)
        dshifted = (dstep_s[...] - rate * ddecay) * logistic(shifted)
        lane = lax.broadcasted_iota(jnp.int32, dshifted.shape, 1)
        dshifted = jnp.where(lane < HEADS, dshifted, 0.0)
        dr_ref[:, WIDE:] = dshifted.astype(bf16)
        late_ref[2, :, 2 * WIDE :] = dshifted.astype(bf16)
        late_ref[3, :, 2 * WIDE :] = jnp.zeros_like(dshifted, bf16)
        headg_ref[...] = jnp.zeros_like(headg_ref)
        headg_ref[0:1, :] = jnp.sum(dshifted, axis=0, keepdims=True)
        headg_ref[1:2, :] = jnp.sum(decay * ddecay, axis=0, keepdims=True)


def whole(shape):
    return pl.BlockSpec(shape, lambda step: (0,) * len(shape))


def columns(rows, start=0):
    return pl.BlockSpec((rows, WIDE), lambda step: (0, start + step))


def fixed_columns(rows, start):
    return pl.BlockSpec((rows, WIDE), lambda step: (0, start))


def shape(rows, cols, dtype=f32):
    return jax.ShapeDtypeStruct((rows, cols), dtype)


def params(mebibytes):
    return pltpu.CompilerParams(dimension_semantics=("arbitrary",), vmem_limit_bytes=mebibytes * 1024 * 1024)


def run_forward(lengths, raw, head, projected, gated_grad, par, gain):
    rows = projected.shape[0]
    state = pltpu.VMEM((STEPS, rows, WIDE), f32)
    narrow = pltpu.VMEM((rows, LANES), f32)
    return pl.pallas_call(
        forward_kernel,
        grid=(STEPS,),
        in_specs=[
            pl.BlockSpec(memory_space=pltpu.SMEM),
            whole((rows, LANES)),
            whole((8, LANES)),
            columns(rows, INNER // WIDE),
            fixed_columns(rows, 2 * INNER // WIDE),
            columns(rows),
            columns(rows),
            columns(8),
            fixed_columns(8, INNER // WIDE),
            whole((1, INNER)),
        ],
        out_specs=[
            whole((rows, INNER)), whole((rows, INNER)), whole((QUARTERS, 2 * rows, 2 * WIDE)), whole((rows, INNER)),
            columns(rows), columns(rows), whole((rows, WIDE)), whole((1, INNER)),
        ],
        out_shape=[
            shape(rows, INNER, bf16), shape(rows, INNER, bf16),
            jax.ShapeDtypeStruct((QUARTERS, 2 * rows, 2 * WIDE), bf16), shape(rows, INNER),
            shape(rows, INNER), shape(rows, INNER), shape(rows, WIDE), shape(1, INNER),
        ],
        scratch_shapes=[
            pltpu.VMEM((CONV_WIDTH - 1, rows, LANES), f32),
            narrow, narrow, pltpu.VMEM((STEPS, 8, rows), f32),
            pltpu.VMEM((2, BLOCK, BLOCK), f32), pltpu.VMEM((BLOCK, BLOCK), bf16),
            state, state, state, state, narrow, narrow,
        ],
        compiler_params=params(28),
        cost_estimate=pl.CostEstimate(flops=15_000_000_000, bytes_accessed=16_000_000, transcendentals=3_000_000),
        name="mixer_forward",
    )(lengths, raw, head, projected, projected, projected, gated_grad, par, par, gain)


def run_backward(lengths, raw, head, projected, conv, convbc, dheads, heads, par):
    rows = projected.shape[0]
    narrow = pltpu.VMEM((rows, LANES), f32)
    square = pltpu.VMEM((2, BLOCK, BLOCK), f32)
    return pl.pallas_call(
        backward_kernel,
        grid=(STEPS,),
        in_specs=[
            pl.BlockSpec(memory_space=pltpu.SMEM),
            whole((rows, LANES)),
            whole((8, LANES)),
            columns(rows, INNER // WIDE),
            fixed_columns(rows, 2 * INNER // WIDE),
            columns(rows), whole((rows, WIDE)), columns(rows), columns(rows),
            columns(8),
            fixed_columns(8, INNER // WIDE),
        ],
        out_specs=[
            columns(rows), whole((rows, WIDE + LANES)), whole((QUARTERS, rows, LATE)), columns(8), whole((8, WIDE)), whole((8, LANES)),
        ],
        out_shape=[
            shape(rows, INNER, bf16), shape(rows, WIDE + LANES, bf16),
            jax.ShapeDtypeStruct((QUARTERS, rows, LATE), bf16), shape(8, INNER), shape(8, WIDE), shape(8, LANES),
        ],
        scratch_shapes=[
            pltpu.VMEM((CONV_WIDTH - 1, rows, LANES), f32),
            narrow, narrow, pltpu.VMEM((STEPS, 8, rows), f32), pltpu.VMEM((rows, WIDE), f32),
            square, pltpu.VMEM((BLOCK, BLOCK), bf16), square, pltpu.VMEM((BLOCK, BLOCK), f32), narrow, narrow,
        ],
        compiler_params=params(20),
        cost_estimate=pl.CostEstimate(flops=20_000_000_000, bytes_accessed=16_000_000, transcendentals=3_000_000),
        name="mixer_backward",
    )(lengths, raw, head, projected, projected, conv, convbc, dheads, heads, par, par)


def normalized(value, gain):
    scale = lax.rsqrt(jnp.mean(value * value, axis=-1, keepdims=True) + epsilon)
    return scale, (value * scale * gain).astype(bf16)


def pack_kernel(len_ref, tokens_ref, cotangent_ref, out_ref):
    rows = tokens_ref.shape[0]
    out_ref[:rows] = tokens_ref[...]
    places = lax.broadcasted_iota(jnp.int32, cotangent_ref.shape, 0)
    total = len_ref[0, 0]
    for slot in range(1, len_ref.shape[1]):
        total = total + len_ref[0, slot]
    out_ref[rows:] = jnp.where(places < total, cotangent_ref[...].astype(f32), 0.0).astype(bf16)


def run_pack(lengths, tokens, cotangent):
    rows, model = tokens.shape
    return pl.pallas_call(
        pack_kernel,
        in_specs=[pl.BlockSpec(memory_space=pltpu.SMEM)] + [pl.BlockSpec(memory_space=pltpu.VMEM)] * 2,
        out_specs=pl.BlockSpec(memory_space=pltpu.VMEM),
        out_shape=shape(2 * rows, model, bf16),
        compiler_params=pltpu.CompilerParams(vmem_limit_bytes=16 * 1024 * 1024),
        cost_estimate=pl.CostEstimate(flops=1, bytes_accessed=2_000_000, transcendentals=0),
        name="known_pack",
    )(lengths, tokens, cotangent)


def known_kernel(core_ref, gain_ref, first, second, third, fourth, mine_ref, theirs_ref, up_ref):
    half = mine_ref.shape[1]
    for at, ref in enumerate((first, second, third, fourth)):
        count = ref.shape[0] // 2
        rows = slice(at * count, (at + 1) * count)
        unused, normed = normalized(ref[:count].astype(f32), gain_ref[...])
        low, high = normed[:, :half], normed[:, half:]
        is_first = core_ref[0] == 0
        mine_ref[rows] = jnp.where(is_first, low, high)
        theirs_ref[rows] = jnp.where(is_first, high, low)
        up_ref[rows] = ref[count:]


def run_known(core, gain, known):
    count, model = known[0].shape[0] // 2, known[0].shape[1]
    every = QUARTERS * count
    return pl.pallas_call(
        known_kernel,
        in_specs=[pl.BlockSpec(memory_space=pltpu.SMEM)] + [pl.BlockSpec(memory_space=pltpu.VMEM)] * 5,
        out_specs=[pl.BlockSpec(memory_space=pltpu.VMEM)] * 3,
        out_shape=[shape(every, model // 2, bf16), shape(every, model // 2, bf16), shape(every, model, bf16)],
        compiler_params=pltpu.CompilerParams(vmem_limit_bytes=32 * 1024 * 1024),
        cost_estimate=pl.CostEstimate(flops=1, bytes_accessed=1, transcendentals=0),
        name="known_rows",
    )(core, gain, *known)


def early_kernel(core_ref, first, second, third, fourth, send_ref, own_ref):
    gate = 2 * WIDE
    for at, ref in enumerate((first, second, third, fourth)):
        count = ref.shape[0] // 2
        rows = slice(at * count, (at + 1) * count)
        low, high = ref[count:, :WIDE], ref[count:, WIDE:]
        is_first = core_ref[0] == 0
        send_ref[rows, :gate] = ref[:count]
        send_ref[rows, gate:] = jnp.where(is_first, high, low)
        own_ref[rows] = jnp.where(is_first, low, high)


def run_early(core, got):
    every = QUARTERS * got[0].shape[0] // 2
    return pl.pallas_call(
        early_kernel,
        in_specs=[pl.BlockSpec(memory_space=pltpu.SMEM)] + [pl.BlockSpec(memory_space=pltpu.VMEM)] * 4,
        out_specs=[pl.BlockSpec(memory_space=pltpu.VMEM)] * 2,
        out_shape=[shape(every, 3 * WIDE, bf16), shape(every, WIDE, bf16)],
        compiler_params=pltpu.CompilerParams(vmem_limit_bytes=32 * 1024 * 1024),
        cost_estimate=pl.CostEstimate(flops=1, bytes_accessed=1, transcendentals=0),
        name="early_factors",
    )(core, *got)


def finish_kernel(side_ref, base_ref, first, first_got, second, second_got, out_ref, rows_s, sems):
    half = first.shape[0] // 2
    body, wide_cols = half - NSTATE, 2 * WIDE
    sizes = [wide_cols] * QUARTERS + [rows_s.shape[0] - INNER]
    moves = [
        pltpu.make_async_copy(
            rows_s.at[pl.ds(at * wide_cols, size)], out_ref.at[pl.ds(INNER + at * wide_cols, size)], sems.at[at]
        )
        for at, size in enumerate(sizes)
    ]
    for place in range(QUARTERS):
        x, y = place // 2, place % 2
        top = slice(y * half, (y + 1) * half)
        start = place * wide_cols
        rows_s[start : start + half] = jnp.where(side_ref[0] == x, first[top], first_got[top]).astype(f32)
        low = slice(x * half, (x + 1) * half)
        value = jnp.where(side_ref[1] == y, second[low], second_got[low]).astype(f32)
        rows_s[start + half : start + wide_cols] = value[:body]
        keep = min(NSTATE, max(0, rows_s.shape[0] - INNER - place * NSTATE))
        if keep:
            rows_s[INNER + place * NSTATE : INNER + place * NSTATE + keep] = value[body : body + keep]
        moves[place].start()
    moves[QUARTERS].start()
    for move in moves:
        move.wait()


def run_finish(sides, base, first, first_got, second, second_got):
    late_rows = base.shape[0] - INNER
    return pl.pallas_call(
        finish_kernel,
        in_specs=[pl.BlockSpec(memory_space=pltpu.SMEM), pl.BlockSpec(memory_space=pl.ANY)]
        + [pl.BlockSpec(memory_space=pltpu.VMEM)] * 4,
        out_specs=pl.BlockSpec(memory_space=pl.ANY),
        out_shape=jax.ShapeDtypeStruct(base.shape, f32),
        scratch_shapes=[pltpu.VMEM((late_rows, base.shape[1]), f32), pltpu.SemaphoreType.DMA((QUARTERS + 1,))],
        input_output_aliases={1: 0},
        compiler_params=pltpu.CompilerParams(vmem_limit_bytes=24 * 1024 * 1024),
        cost_estimate=pl.CostEstimate(flops=1, bytes_accessed=8_000_000, transcendentals=0),
        name="late_rows",
    )(sides, base, first, first_got, second, second_got)


def make_shards(mesh):
    reps = mesh.shape["rep"]
    bits = reps.bit_length() - 1
    assert reps == 1 << bits and bits >= 2 and mesh.shape["shard"] == 2
    up_order, down_order = tuple(range(2, bits)), tuple(reversed(range(2, bits)))
    far = len(up_order)

    def swap(value):
        return lax.ppermute(value, "shard", [(0, 1), (1, 0)])

    def across(value, flip):
        return lax.ppermute(value, "rep", [(place, place ^ flip) for place in range(reps)])

    def side_of(bit):
        return (lax.axis_index("rep") >> bit) & 1

    def quarter_of(flip):
        place = lax.axis_index("rep") ^ flip
        return (place & 1) * 2 + ((place >> 1) & 1)

    def joined(side, mine, theirs, axis):
        return jnp.where(
            side == 0, jnp.concatenate([mine, theirs], axis=axis), jnp.concatenate([theirs, mine], axis=axis)
        )

    def part(value, bit, flip):
        half = value.shape[0] // 2
        return lax.dynamic_slice_in_dim(value, (side_of(bit) ^ flip) * half, half)

    def terms(smalls):
        high = lax.reduce_precision(smalls, 8, 7)
        return jnp.concatenate([high.astype(bf16), (smalls - high).astype(bf16)], axis=0)

    def exchange(value, bit, smalls):
        if smalls is None:
            return across(value, 1 << bit), None
        rows, count = value.shape[0], smalls.shape[0]
        got = across(jnp.concatenate([value, terms(smalls)], axis=0), 1 << bit)
        added = got[rows:].astype(f32)
        return got[:rows], smalls + added[:count] + added[count:]

    def scatter(value, bit, smalls=None):
        got, smalls = exchange(part(value, bit, 1).astype(bf16), bit, smalls)
        return part(value, bit, 0) + got.astype(f32), smalls

    def gather(value, bit, smalls=None):
        got, smalls = exchange(value, bit, smalls)
        return joined(side_of(bit), value, got, 0), smalls

    def pair_step(pieces, at, smalls=None, carrier=1):
        beside = [None, None]
        beside[carrier] = smalls
        moved = []
        for which, value in enumerate(pieces):
            order = (up_order, down_order)[which]
            if at < far:
                moved.append(scatter(value, order[at], beside[which]))
            else:
                value = value.astype(bf16) if at == far else value
                late_at = at - 2 * far
                bit = order[2 * far - 1 - at] if late_at < 0 else (1 - late_at, late_at)[which]
                moved.append(gather(value, bit, beside[which]))
        return tuple(value for value, _ in moved), moved[carrier][1]

    steps = 2 * far + 2

    def turned(value):
        size = value.shape[0] // QUARTERS
        return [value[at * size : (at + 1) * size] for at in (0, 2, 1, 3)]

    def shards(
        tokens, lengths, norm_gain, in_weight, conv_weight, conv_bias, step_bias, decay_log, skip_gain,
        gate_gain, out_weight, cotangent,
    ):
        core = lax.axis_index("shard")
        rows, model = tokens.shape
        half_model, half_inner = model // 2, INNER // 2
        half_conv, half_heads = CONVDIM // 2, HEADS // 2

        def mine(value, size):
            return lax.dynamic_slice_in_dim(value, core * size, size, axis=1)

        def theirs(value, size):
            return lax.dynamic_slice_in_dim(value, (1 - core) * size, size, axis=1)

        known = run_pack(lengths, tokens, cotangent)
        upstream = known[rows:]
        known = [known, *(across(known, flip) for flip in (1, 2, 3))]

        def line(value):
            return jnp.pad(value, (0, half_conv - value.shape[0]))[None]

        small = jnp.concatenate(
            [
                conv_weight.T, conv_bias[None], line(gate_gain),
                line(jnp.concatenate([norm_gain, step_bias, decay_log, skip_gain])),
                jnp.zeros((1, half_conv), bf16),
            ],
            axis=0,
        )
        small_o = swap(small)
        in_other = swap(in_weight)
        out_other = swap(out_weight)
        small, small_o = small.astype(f32), small_o.astype(f32)
        low_half, high_half = jnp.where(core == 0, small, small_o), jnp.where(core == 0, small_o, small)
        both = jnp.concatenate([low_half, high_half], axis=1)

        def pick(row, start, size):
            return jnp.concatenate([low_half[row, start : start + size], high_half[row, start : start + size]])

        norm_scale = pick(6, 0, half_model)
        head_lines = [pick(6, half_model + at * half_heads, half_heads) for at in range(3)]
        gate_line = pick(5, 0, half_inner)[None]
        par = jnp.concatenate(
            [
                both[:5],
                jnp.pad(gate_line, ((0, 0), (0, CONVDIM - INNER))),
                jnp.pad(jnp.repeat(head_lines[2], HEADDIM)[None], ((0, 0), (0, CONVDIM - INNER))),
                jnp.zeros((1, CONVDIM), f32),
            ],
            axis=0,
        )
        head = jnp.pad(jnp.stack(head_lines[:2]), ((0, 6), (0, LANES - HEADS)))

        inputs = tokens.astype(f32)
        scale, normed = normalized(inputs, norm_scale)
        normed_m, normed_o = mine(normed, half_model), theirs(normed, half_model)

        gated_grad = joined(core, mm(upstream, out_weight, LANE), mm(upstream, out_other, LANE), 1)
        projected = mm(normed_m, in_weight) + mm(normed_o, in_other)
        raw = jnp.pad(projected[:, STEP_COL:], ((0, 0), (0, LANES - HEADS)))
        gated, dgate, leaving, dheads, heads, conv, convbc, gain_g = run_forward(
            lengths, raw, head, projected, gated_grad, par, gate_line
        )

        def quarters(value):
            return [lax.dynamic_index_in_dim(value, quarter_of(flip), 0, keepdims=False) for flip in range(QUARTERS)]

        early_sent = quarters(leaving)
        early_got = [early_sent[0], *(across(early_sent[flip], flip) for flip in (1, 2, 3))]
        dx, dr, late, par_g, parbc_g, head_g = run_backward(
            lengths, raw, head, projected, conv, convbc, dheads, heads, par
        )

        late_sent = quarters(late)
        late_sent, known = lax.optimization_barrier((late_sent, known))
        place = core.astype(jnp.int32)[None]
        known_m, known_t, known_up = run_known(place, norm_scale[None], known)
        known_o, known_up_o = swap(known_t), swap(known_up)
        gated_m, gated_o = mine(gated, half_inner), theirs(gated, half_inner)
        branch = mm(gated_m, out_weight) + mm(gated_o, out_other)
        live = (jnp.arange(rows, dtype=jnp.int32) < jnp.sum(lengths))[:, None]
        output = (inputs + jnp.where(live, branch, 0.0)).astype(bf16)
        proj_grad = jnp.concatenate([dgate, dx, dr[:, : CONVDIM - INNER + HEADS]], axis=1)
        normed_grad = joined(core, mm(proj_grad, in_weight, LANE), mm(proj_grad, in_other, LANE), 1)
        g = normed_grad * norm_scale
        input_grad = (
            cotangent.astype(f32)
            + scale * g
            - inputs * (scale * scale * scale * jnp.mean(g * inputs, axis=-1, keepdims=True))
        )
        gain_grad = jnp.sum(normed_grad * inputs * scale, axis=0)

        skip_g = jnp.sum(par_g[6].reshape(HEADS, HEADDIM), axis=1)
        tail = jnp.concatenate([gain_grad, head_g[0, :HEADS], head_g[1, :HEADS], skip_g])
        total = jnp.concatenate(
            [
                jnp.concatenate([par_g[:5], parbc_g[:5]], axis=1),
                jnp.pad(gain_g, ((0, 0), (0, CONVDIM - INNER))),
                jnp.pad(tail, (0, CONVDIM - tail.shape[0]))[None],
                jnp.zeros((1, CONVDIM), f32),
            ],
            axis=0,
        )
        smalls = (total + swap(total)).reshape(-1, half_model)
        early_got, output, input_grad, smalls = lax.optimization_barrier((early_got, output, input_grad, smalls))
        late_got = [late_sent[0], *(across(late_sent[flip], flip) for flip in (1, 2, 3))]
        early_m, early_out_m = run_early(place, early_got)
        early_o = swap(early_m)
        gate_cols = 2 * WIDE
        early = (
            mm(early_out_m, known_up, ROWS) + mm(early_o[:, gate_cols:], known_up_o, ROWS),
            mm(early_m[:, :gate_cols], known_m, ROWS) + mm(early_o[:, :gate_cols], known_o, ROWS),
        )
        early, _ = pair_step(early, 0)
        early, _ = pair_step(early, 1)
        early, late_got = lax.optimization_barrier((early, late_got))
        early, _ = pair_step(early, 2)
        late_all = jnp.concatenate(late_got, axis=0)
        late_all_o = swap(late_all)
        early, late_all, late_all_o = lax.optimization_barrier((early, late_all, late_all_o))
        early, _ = pair_step(early, 3)
        late_grad = mm(late_all, known_m, ROWS) + mm(late_all_o, known_o, ROWS)
        early, late_grad = lax.optimization_barrier((early, late_grad))
        half_late = LATE // 2
        late_parts = (late_grad[:half_late], late_grad[half_late:])
        last = 2 * far + 1
        last = 2 * far + 1
        for at in range(4, steps):
            early, smalls = pair_step(early, at, smalls) if at == last - 1 else (pair_step(early, at)[0], smalls)
            for late_at in {last - 1: range(far), last: range(far, 2 * far)}.get(at, ()):
                late_parts, added = pair_step(late_parts, late_at, smalls if late_at >= far else None)
                smalls = smalls if added is None else added
            if at >= last:
                early, late_parts = lax.optimization_barrier((early, late_parts))
        late_parts, smalls = pair_step(late_parts, steps - 2, smalls, 0)
        out_grad = early[0].astype(f32)
        late_parts, out_grad = lax.optimization_barrier((late_parts, out_grad))
        in_grad = jnp.concatenate(
            [*turned(early[1]), jnp.zeros((STEP_COL + HEADS - INNER, half_model), bf16)], axis=0
        ).astype(f32)
        total = smalls.reshape(total.shape)

        def own(row, start, size):
            return lax.dynamic_slice_in_dim(total[row], start + core * size, size)

        small_grads = (
            own(6, 0, half_model),
            lax.dynamic_slice_in_dim(total[:4], core * half_conv, half_conv, axis=1).T,
            own(4, 0, half_conv),
            own(6, model, half_heads),
            own(6, model + HEADS, half_heads),
            own(6, model + 2 * HEADS, half_heads),
            own(5, 0, half_inner),
        )
        in_grad, small_grads = lax.optimization_barrier((in_grad, small_grads))
        sides = jnp.stack([side_of(0), side_of(1)]).astype(jnp.int32)
        in_grad = run_finish(
            sides, in_grad, late_parts[0], across(late_parts[0], 1), late_parts[1], across(late_parts[1], 2)
        ).T
        norm_grad, conv_grad, bias_grad, step_grad, decay_grad, skip_grad, gate_grad = small_grads

        return (
            output, input_grad, norm_grad, in_grad, conv_grad, bias_grad, step_grad, decay_grad, skip_grad,
            gate_grad, out_grad,
        )

    return shards


def solution(mesh):
    split = P(("rep", "shard"), None)
    vector, matrix = P("shard"), P("shard", None)
    in_specs = (
        split, split, vector, matrix, matrix, vector, vector, vector, vector, vector, matrix, split,
    )
    out_specs = (
        split, split, vector, matrix, matrix, vector, vector, vector, vector, vector, matrix,
    )
    return jax.shard_map(make_shards(mesh), mesh=mesh, in_specs=in_specs, out_specs=out_specs, check_vma=False)
```

```python
import jax
import jax.numpy as jnp
from jax import lax
from jax.experimental import pallas as pl
from jax.experimental.pallas import tpu as pltpu
from jax.sharding import PartitionSpec as P

HEADS = 32
HEADDIM = 64
NSTATE = 128
CONV_WIDTH = 4
BLOCK = 128
INNER = 2048
CONVDIM = 2304
STEP_COL = INNER + CONVDIM

GROUP = 4
WIDE = GROUP * HEADDIM
STEPS = HEADS // GROUP
QUARTERS = 4
LATE = INNER // QUARTERS + NSTATE
LANES = 128
HEAD_SUMS = 1024

epsilon = 1e-05
highest = lax.Precision.HIGHEST
f32 = jnp.float32
bf16 = jnp.bfloat16


def mm(left, right, dims=((1,), (0,)), precision=None):
    return lax.dot_general(left, right, (dims, ((), ())), precision=precision, preferred_element_type=f32)


LANE = ((1,), (1,))
ROWS = ((0,), (0,))


def segment_of(places, len_ref):
    end = len_ref[0, 0]
    segment = (places >= end).astype(jnp.int32)
    for slot in range(1, len_ref.shape[1]):
        end = end + len_ref[0, slot]
        segment = segment + (places >= end).astype(jnp.int32)
    return segment


def write_joined(len_ref, joined_ref):
    rows, lanes = joined_ref.shape[1:]
    places = lax.broadcasted_iota(jnp.int32, (rows, lanes), 0)
    segment = segment_of(places, len_ref)
    for offset in range(1, CONV_WIDTH):
        same = (segment_of(places - offset, len_ref) == segment) & (places >= offset)
        joined_ref[offset - 1] = same.astype(f32)


def wide(mask):
    return jnp.concatenate([mask, mask], axis=1)


def linked(len_ref, row_start, col_start):
    rows = lax.broadcasted_iota(jnp.int32, (BLOCK, BLOCK), 0) + row_start
    cols = lax.broadcasted_iota(jnp.int32, (BLOCK, BLOCK), 1) + col_start
    return (segment_of(rows, len_ref) == segment_of(cols, len_ref)) & (rows >= cols)


def step_terms(raw_ref, head_ref):
    lane = lax.broadcasted_iota(jnp.int32, raw_ref.shape, 1)
    shifted = jnp.where(lane < HEADS, raw_ref[...] + head_ref[0:1, :], 0.0)
    step = jnp.maximum(shifted, 0.0) + jnp.log1p(jnp.exp(-jnp.abs(shifted)))
    rate = jnp.exp(head_ref[1:2, :])
    return shifted, step, rate, -step * rate


def lower():
    rows = lax.broadcasted_iota(jnp.int32, (BLOCK, BLOCK), 0)
    cols = lax.broadcasted_iota(jnp.int32, (BLOCK, BLOCK), 1)
    return (rows >= cols).astype(f32)


def write_running(raw_ref, head_ref, step_ref, run_ref, runt_ref):
    unused, step, rate, decay = step_terms(raw_ref, head_ref)
    step_ref[...] = step
    for block in range(2):
        rows = slice(block * BLOCK, (block + 1) * BLOCK)
        running = mm(lower(), decay[rows], precision=highest)
        run_ref[rows, :] = running
        turned = running.T
        for group in range(STEPS):
            runt_ref[group, 0:GROUP, rows] = turned[group * GROUP : (group + 1) * GROUP]


def conv_silu(signal, par, joined_ref):
    summed = par[4:5] + signal * par[3:4]
    for offset in range(1, CONV_WIDTH):
        tap = par[3 - offset : 4 - offset]
        summed = summed + pltpu.roll(signal, offset, 0) * wide(joined_ref[offset - 1]) * tap
    return summed


def conv_back(grad, signal, par, joined_ref, store):
    rows = grad.shape[0]
    back = grad * par[3:4]
    store(3, jnp.sum(grad * signal, axis=0, keepdims=True))
    store(4, jnp.sum(grad, axis=0, keepdims=True))
    for offset in range(1, CONV_WIDTH):
        masked = grad * wide(joined_ref[offset - 1])
        store(3 - offset, jnp.sum(masked * pltpu.roll(signal, offset, 0), axis=0, keepdims=True))
        back = back + pltpu.roll(masked, rows - offset, 0) * par[3 - offset : 4 - offset]
    return back


def logistic(value):
    return 0.5 * jnp.tanh(0.5 * value) + 0.5


def head_columns(table, step):
    return pltpu.roll(table, lax.rem(LANES - GROUP * step, LANES), 1)


def spread(columns, head):
    return jnp.broadcast_to(columns[:, head : head + 1], (columns.shape[0], LANES))


def half_lanes(shape):
    return lax.broadcasted_iota(jnp.int32, shape, 1) < HEADDIM


def decay_pair(pair, block, runs, runt_ref, step):
    rows = slice(block * BLOCK, (block + 1) * BLOCK)
    out = []
    for place in (2 * pair, 2 * pair + 1):
        row = runt_ref[step, place : place + 1, rows]
        out.append(jnp.exp(jnp.minimum(runs[place][rows] - row, 0.0)))
    return out


def split_heads(value):
    first = half_lanes(value.shape)
    zero = jnp.zeros_like(value)
    return jnp.concatenate([jnp.where(first, value, zero), jnp.where(first, zero, value)], axis=0)


def pair_terms(pair, runs, steps):
    first = half_lanes(runs[0].shape)
    run = jnp.where(first, runs[2 * pair], runs[2 * pair + 1])
    step = jnp.where(first, steps[2 * pair], steps[2 * pair + 1])
    into = jnp.exp(run[BLOCK:])
    toward = jnp.exp(run[BLOCK - 1 : BLOCK] - run[:BLOCK])
    return step, into, toward


def forward_kernel(
    len_ref, raw_ref, head_ref, sig_ref, bc_ref, gate_ref, grad_ref, par_ref, parbc_ref, gain_ref,
    gated_ref, dgate_ref, sent_ref, dheads_ref, heads_ref, conv_ref, convbc_ref, gaing_ref,
    joined, step_s, run_s, runt_s, score_s, cross_s, u_s, silu_s, slope_s, grad_s, sq_s, mix_s,
):
    step = pl.program_id(0)

    @pl.when(step == 0)
    def prepare():
        write_joined(len_ref, joined)
        write_running(raw_ref, head_ref, step_s, run_s, runt_s)
        summed = conv_silu(bc_ref[...], parbc_ref[...], joined)
        convbc_ref[...] = summed
        active = summed * logistic(summed)
        write_map, read_map = active[:, :NSTATE], active[:, NSTATE:]
        for block in range(2):
            rows = slice(block * BLOCK, (block + 1) * BLOCK)
            scores = mm(read_map[rows], write_map[rows], LANE, highest)
            score_s[block] = jnp.where(linked(len_ref, block * BLOCK, block * BLOCK), scores, 0.0)
        cross = mm(read_map[BLOCK:], write_map[:BLOCK], LANE, highest)
        cross_s[...] = jnp.where(linked(len_ref, BLOCK, 0), cross, 0.0).astype(bf16)
        sq_s[...] = jnp.zeros_like(sq_s)
        mix_s[...] = jnp.zeros_like(mix_s)

    par = par_ref[...]
    summed = conv_silu(sig_ref[...], par, joined)
    conv_ref[...] = summed
    head_in = summed * logistic(summed)
    run_cols = head_columns(run_s[...], step)
    step_cols = head_columns(step_s[...], step)
    runs = [spread(run_cols, head) for head in range(GROUP)]
    steps = [spread(step_cols, head) for head in range(GROUP)]
    tops, bottoms, intos, sources = [], [], [], []
    for pair in range(GROUP // 2):
        lanes = slice(pair * LANES, (pair + 1) * LANES)
        step_size, into, toward = pair_terms(pair, runs, steps)
        scaled = head_in[:, lanes] * step_size
        low = scaled.astype(bf16)
        for block, found in ((0, tops), (1, bottoms)):
            rows = slice(block * BLOCK, (block + 1) * BLOCK)
            first, second = decay_pair(pair, block, runs, runt_s, step)
            mixing = jnp.concatenate([first * score_s[block], second * score_s[block]], axis=1)
            found.append(mm(mixing.astype(bf16), split_heads(low[rows])))
        intos.append(into)
        sources.append((scaled[:BLOCK] * toward).astype(bf16))
    carried = mm(cross_s[...], jnp.concatenate(sources, axis=1)) * jnp.concatenate(intos, axis=1)
    top, bottom = jnp.concatenate(tops, axis=1), jnp.concatenate(bottoms, axis=1)
    heads_ref[:BLOCK] = top
    heads_ref[BLOCK:] = bottom
    heads = jnp.concatenate([top, bottom + carried], axis=0) + par[6:7] * head_in
    gate = gate_ref[...]
    opened = logistic(gate)
    silu = gate * opened
    u = heads * silu
    grad = grad_ref[...]
    mixed = grad * par[5:6] * u
    square = u * u
    sq_s[...] += square[:, :LANES] + square[:, LANES:]
    mix_s[...] += mixed[:, :LANES] + mixed[:, LANES:]
    u_s[step] = u
    silu_s[step] = silu
    slope_s[step] = heads * (opened * (1.0 + gate * (1.0 - opened)))
    grad_s[step] = grad

    @pl.when(step == STEPS - 1)
    def finish():
        scale = lax.rsqrt(jnp.sum(sq_s[...], axis=1, keepdims=True) * (1.0 / INNER) + epsilon)
        rows = scale.shape[0]
        drag = scale * scale * scale * (jnp.sum(mix_s[...], axis=1, keepdims=True) * (1.0 / INNER))
        for part in range(STEPS):
            lanes = slice(part * WIDE, (part + 1) * WIDE)
            gain = gain_ref[:, lanes]
            normal = u_s[part] * scale
            grad = grad_s[part]
            gated = (normal * gain).astype(bf16)
            gated_ref[:, lanes] = gated
            core, place = part // QUARTERS, part % QUARTERS
            sent_ref[place, rows:, core * WIDE : (core + 1) * WIDE] = gated
            gaing_ref[:, lanes] = jnp.sum(grad * normal, axis=0, keepdims=True)
            du = scale * (grad * gain) - u_s[part] * drag
            dheads_ref[:, lanes] = du * silu_s[part]
            dgate = (du * slope_s[part]).astype(bf16)
            dgate_ref[:, lanes] = dgate
            half = part % 2
            sent_ref[part // 2, :rows, half * WIDE : (half + 1) * WIDE] = dgate


def backward_kernel(
    len_ref, raw_ref, head_ref, sig_ref, bc_ref, conv_ref, convbc_ref, dheads_ref, heads_ref, par_ref, parbc_ref,
    gaing_ref, dx_ref, dr_ref, late_ref, total_ref,
    joined, step_s, run_s, runt_s, maps_s, score_s, cross_s, dscore_s, dcross_s, dstep_s, ddecay_s, dskip_s,
):
    step = pl.program_id(0)

    @pl.when(step == 0)
    def prepare():
        write_joined(len_ref, joined)
        write_running(raw_ref, head_ref, step_s, run_s, runt_s)
        summed = convbc_ref[...]
        active = summed * logistic(summed)
        maps_s[...] = active
        write_map, read_map = active[:, :NSTATE], active[:, NSTATE:]
        for block in range(2):
            rows = slice(block * BLOCK, (block + 1) * BLOCK)
            scores = mm(read_map[rows], write_map[rows], LANE, highest)
            score_s[block] = jnp.where(linked(len_ref, block * BLOCK, block * BLOCK), scores, 0.0)
        cross = mm(read_map[BLOCK:], write_map[:BLOCK], LANE, highest)
        cross_s[...] = jnp.where(linked(len_ref, BLOCK, 0), cross, 0.0).astype(bf16)
        dscore_s[...] = jnp.zeros_like(dscore_s)
        dcross_s[...] = jnp.zeros_like(dcross_s)
        dstep_s[...] = jnp.zeros_like(dstep_s)
        ddecay_s[...] = jnp.zeros_like(ddecay_s)
        dskip_s[...] = jnp.zeros_like(dskip_s)
        total_ref[...] = jnp.zeros_like(total_ref)
        total_ref[5:6, :INNER] = gaing_ref[...]

    par = par_ref[...]
    summed = conv_ref[...]
    opened = logistic(summed)
    head_in = summed * opened
    slope = opened * (1.0 + summed * (1.0 - opened))
    run_cols = head_columns(run_s[...], step)
    step_cols = head_columns(step_s[...], step)
    runs = [spread(run_cols, head) for head in range(GROUP)]
    steps = [spread(step_cols, head) for head in range(GROUP)]
    dheads = dheads_ref[...]
    dlow = dheads.astype(bf16)
    tops, bottoms, towards, sinks, sources, lows, sizes = [], [], [], [], [], [], []
    for pair in range(GROUP // 2):
        lanes = slice(pair * LANES, (pair + 1) * LANES)
        step_size, into, toward = pair_terms(pair, runs, steps)
        scaled = head_in[:, lanes] * step_size
        low = scaled.astype(bf16)
        for block, found in ((0, tops), (1, bottoms)):
            rows = slice(block * BLOCK, (block + 1) * BLOCK)
            first, second = decay_pair(pair, block, runs, runt_s, step)
            mixing = jnp.concatenate([first * score_s[block], second * score_s[block]], axis=0)
            parted = split_heads(dlow[rows, lanes])
            found.append(mm(mixing.astype(bf16), parted, ROWS))
            dmixing = mm(parted, low[rows], LANE)
            dscore_s[block] += first * dmixing[:BLOCK] + second * dmixing[BLOCK:]
        sinks.append((dheads[BLOCK:, lanes] * into).astype(bf16))
        sources.append((scaled[:BLOCK] * toward).astype(bf16))
        towards.append(toward)
        lows.append(low)
        sizes.append(step_size)
    sink, source = jnp.concatenate(sinks, axis=1), jnp.concatenate(sources, axis=1)
    dcross_s[...] += mm(sink, source, LANE)
    arrived, returned = mm(cross_s[...], source), mm(cross_s[...], sink, ROWS)
    inside = jnp.concatenate([jnp.concatenate(tops, axis=1), jnp.concatenate(bottoms, axis=1)], axis=0)
    dscaled = jnp.concatenate(
        [inside[:BLOCK] + returned * jnp.concatenate(towards, axis=1), inside[BLOCK:]], axis=0
    )
    between = jnp.concatenate([-source.astype(f32) * returned, sink.astype(f32) * arrived], axis=0)
    owner = lax.broadcasted_iota(jnp.int32, (WIDE, LANES), 0) // HEADDIM + GROUP * step
    sums = (owner == lax.broadcasted_iota(jnp.int32, (WIDE, LANES), 1)).astype(f32)
    low = jnp.concatenate(lows, axis=1).astype(f32)
    moved = dlow.astype(f32) * heads_ref[...] - low * inside + between
    ddecay_s[...] += mm(moved, sums, precision=highest)
    dstep_s[...] += mm(head_in * dscaled, sums, precision=highest)
    dhead_in = jnp.concatenate(sizes, axis=1) * dscaled + par[6:7] * dheads

    def store(row, value):
        total_ref[row : row + 1, pl.ds(pl.multiple_of(step * WIDE, WIDE), WIDE)] = value

    dskip = jnp.broadcast_to(jnp.sum(dheads * head_in, axis=0, keepdims=True), (8, WIDE))
    dskip_s[...] += mm(dskip, sums, precision=highest)
    dx = conv_back(dhead_in * slope, sig_ref[...], par, joined, store).astype(bf16)
    dx_ref[...] = dx
    late_ref[step // 2, :, pl.ds(pl.multiple_of(lax.rem(step, 2) * WIDE, WIDE), WIDE)] = dx

    @pl.when(step == STEPS - 1)
    def finish():
        maps = maps_s[...]
        write_map, read_map = maps[:, :NSTATE], maps[:, NSTATE:]
        w0, w1, r0, r1 = write_map[:BLOCK], write_map[BLOCK:], read_map[:BLOCK], read_map[BLOCK:]
        d0 = jnp.where(linked(len_ref, 0, 0), dscore_s[0], 0.0)
        d1 = jnp.where(linked(len_ref, BLOCK, BLOCK), dscore_s[1], 0.0)
        dc = jnp.where(linked(len_ref, BLOCK, 0), dcross_s[...], 0.0)
        dread = jnp.concatenate(
            [mm(d0, w0, precision=highest), mm(d1, w1, precision=highest) + mm(dc, w0, precision=highest)], axis=0
        )
        dwrite = jnp.concatenate(
            [mm(d0, r0, ROWS, highest) + mm(dc, r1, ROWS, highest), mm(d1, r1, ROWS, highest)], axis=0
        )
        summed = convbc_ref[...]
        opened = logistic(summed)
        slope = opened * (1.0 + summed * (1.0 - opened))

        def store(row, value):
            total_ref[row : row + 1, INNER:] = value

        grad = jnp.concatenate([dwrite, dread], axis=1) * slope
        dmaps = conv_back(grad, bc_ref[...], parbc_ref[...], joined, store).astype(bf16)
        dr_ref[:, :WIDE] = dmaps
        late_ref[0, :, 2 * WIDE :] = dmaps[:, :NSTATE]
        late_ref[1, :, 2 * WIDE :] = dmaps[:, NSTATE:]

        shifted, step_size, rate, decay = step_terms(raw_ref, head_ref)
        change = ddecay_s[...]
        late = mm(lower(), change[BLOCK:], ROWS, highest)
        early = mm(lower(), change[:BLOCK], ROWS, highest) + late[0:1]
        ddecay = jnp.concatenate([early, late], axis=0)
        dshifted = (dstep_s[...] - rate * ddecay) * logistic(shifted)
        lane = lax.broadcasted_iota(jnp.int32, dshifted.shape, 1)
        dshifted = jnp.where(lane < HEADS, dshifted, 0.0)
        dr_ref[:, WIDE:] = dshifted.astype(bf16)
        late_ref[2, :, 2 * WIDE :] = dshifted.astype(bf16)
        late_ref[3, :, 2 * WIDE :] = jnp.zeros_like(dshifted, bf16)
        head_sums = (
            jnp.sum(dshifted, axis=0, keepdims=True),
            jnp.sum(decay * ddecay, axis=0, keepdims=True),
            dskip_s[0:1, :],
        )
        for at, sums_of in enumerate(head_sums):
            total_ref[6:7, HEAD_SUMS + at * LANES : HEAD_SUMS + (at + 1) * LANES] = sums_of


def whole(shape):
    return pl.BlockSpec(shape, lambda step: (0,) * len(shape))


def columns(rows, start=0):
    return pl.BlockSpec((rows, WIDE), lambda step: (0, start + step))


def fixed_columns(rows, start):
    return pl.BlockSpec((rows, WIDE), lambda step: (0, start))


def shape(rows, cols, dtype=f32):
    return jax.ShapeDtypeStruct((rows, cols), dtype)


def params(mebibytes):
    return pltpu.CompilerParams(dimension_semantics=("arbitrary",), vmem_limit_bytes=mebibytes * 1024 * 1024)


def run_forward(lengths, raw, head, projected, gated_grad, par, gain):
    rows = projected.shape[0]
    state = pltpu.VMEM((STEPS, rows, WIDE), f32)
    narrow = pltpu.VMEM((rows, LANES), f32)
    return pl.pallas_call(
        forward_kernel,
        grid=(STEPS,),
        in_specs=[
            pl.BlockSpec(memory_space=pltpu.SMEM),
            whole((rows, LANES)),
            whole((8, LANES)),
            columns(rows, INNER // WIDE),
            fixed_columns(rows, 2 * INNER // WIDE),
            columns(rows),
            columns(rows),
            columns(8),
            fixed_columns(8, INNER // WIDE),
            whole((1, INNER)),
        ],
        out_specs=[
            whole((rows, INNER)), whole((rows, INNER)), whole((QUARTERS, 2 * rows, 2 * WIDE)), whole((rows, INNER)),
            columns(rows), columns(rows), whole((rows, WIDE)), whole((1, INNER)),
        ],
        out_shape=[
            shape(rows, INNER, bf16), shape(rows, INNER, bf16),
            jax.ShapeDtypeStruct((QUARTERS, 2 * rows, 2 * WIDE), bf16), shape(rows, INNER),
            shape(rows, INNER), shape(rows, INNER), shape(rows, WIDE), shape(1, INNER),
        ],
        scratch_shapes=[
            pltpu.VMEM((CONV_WIDTH - 1, rows, LANES), f32),
            narrow, narrow, pltpu.VMEM((STEPS, 8, rows), f32),
            pltpu.VMEM((2, BLOCK, BLOCK), f32), pltpu.VMEM((BLOCK, BLOCK), bf16),
            state, state, state, state, narrow, narrow,
        ],
        compiler_params=params(25),
        cost_estimate=pl.CostEstimate(flops=15_000_000_000, bytes_accessed=16_000_000, transcendentals=3_000_000),
        name="mixer_forward",
    )(lengths, raw, head, projected, projected, projected, gated_grad, par, par, gain)


def run_backward(lengths, raw, head, projected, conv, convbc, dheads, heads, par, gain_g):
    rows = projected.shape[0]
    narrow = pltpu.VMEM((rows, LANES), f32)
    square = pltpu.VMEM((2, BLOCK, BLOCK), f32)
    return pl.pallas_call(
        backward_kernel,
        grid=(STEPS,),
        in_specs=[
            pl.BlockSpec(memory_space=pltpu.SMEM),
            whole((rows, LANES)),
            whole((8, LANES)),
            columns(rows, INNER // WIDE),
            fixed_columns(rows, 2 * INNER // WIDE),
            columns(rows), whole((rows, WIDE)), columns(rows), columns(rows),
            columns(8),
            fixed_columns(8, INNER // WIDE),
            whole((1, INNER)),
        ],
        out_specs=[
            columns(rows), whole((rows, WIDE + LANES)), whole((QUARTERS, rows, LATE)), whole((8, CONVDIM)),
        ],
        out_shape=[
            shape(rows, INNER, bf16), shape(rows, WIDE + LANES, bf16),
            jax.ShapeDtypeStruct((QUARTERS, rows, LATE), bf16), shape(8, CONVDIM),
        ],
        scratch_shapes=[
            pltpu.VMEM((CONV_WIDTH - 1, rows, LANES), f32),
            narrow, narrow, pltpu.VMEM((STEPS, 8, rows), f32), pltpu.VMEM((rows, WIDE), f32),
            square, pltpu.VMEM((BLOCK, BLOCK), bf16), square, pltpu.VMEM((BLOCK, BLOCK), f32), narrow, narrow,
            pltpu.VMEM((8, LANES), f32),
        ],
        compiler_params=params(12),
        cost_estimate=pl.CostEstimate(flops=20_000_000_000, bytes_accessed=16_000_000, transcendentals=3_000_000),
        name="mixer_backward",
    )(lengths, raw, head, projected, projected, conv, convbc, dheads, heads, par, par, gain_g)


def normalized(value, gain):
    scale = lax.rsqrt(jnp.mean(value * value, axis=-1, keepdims=True) + epsilon)
    return scale, (value * scale * gain).astype(bf16)


def pack_kernel(len_ref, tokens_ref, cotangent_ref, out_ref):
    rows = tokens_ref.shape[0]
    out_ref[:rows] = tokens_ref[...]
    places = lax.broadcasted_iota(jnp.int32, cotangent_ref.shape, 0)
    total = len_ref[0, 0]
    for slot in range(1, len_ref.shape[1]):
        total = total + len_ref[0, slot]
    out_ref[rows:] = jnp.where(places < total, cotangent_ref[...].astype(f32), 0.0).astype(bf16)


def run_pack(lengths, tokens, cotangent):
    rows, model = tokens.shape
    return pl.pallas_call(
        pack_kernel,
        in_specs=[pl.BlockSpec(memory_space=pltpu.SMEM)] + [pl.BlockSpec(memory_space=pltpu.VMEM)] * 2,
        out_specs=pl.BlockSpec(memory_space=pltpu.VMEM),
        out_shape=shape(2 * rows, model, bf16),
        compiler_params=pltpu.CompilerParams(vmem_limit_bytes=16 * 1024 * 1024),
        cost_estimate=pl.CostEstimate(flops=1, bytes_accessed=2_000_000, transcendentals=0),
        name="known_pack",
    )(lengths, tokens, cotangent)


def known_kernel(gain_ref, first, second, third, fourth, normed_ref, up_ref):
    for at, ref in enumerate((first, second, third, fourth)):
        count = ref.shape[0] // 2
        rows = slice(at * count, (at + 1) * count)
        unused, normed_ref[rows] = normalized(ref[:count].astype(f32), gain_ref[...])
        up_ref[rows] = ref[count:]


def run_known(gain, known):
    every, model = QUARTERS * known[0].shape[0] // 2, known[0].shape[1]
    return pl.pallas_call(
        known_kernel,
        in_specs=[pl.BlockSpec(memory_space=pltpu.VMEM)] * 5,
        out_specs=[pl.BlockSpec(memory_space=pltpu.VMEM)] * 2,
        out_shape=[shape(every, model, bf16)] * 2,
        compiler_params=pltpu.CompilerParams(vmem_limit_bytes=24 * 1024 * 1024),
        cost_estimate=pl.CostEstimate(flops=1, bytes_accessed=1, transcendentals=0),
        name="known_rows",
    )(gain, *known)


def parted(core_ref, low, high, mine_ref, theirs_ref):
    is_first = core_ref[0] == 0
    mine_ref[...] = jnp.where(is_first, low, high)
    theirs_ref[...] = jnp.where(is_first, high, low).astype(bf16)


def early_kernel(core_ref, normed_ref, up_ref, *refs):
    got, (gate_ref, gate_o_ref, out_ref, out_o_ref) = refs[:QUARTERS], refs[QUARTERS:]
    count = got[0].shape[0] // 2
    gate = mm(jnp.concatenate([ref[:count] for ref in got], axis=0), normed_ref[...], ROWS)
    half = gate_ref.shape[1]
    parted(core_ref, gate[:, :half], gate[:, half:], gate_ref, gate_o_ref)
    out = mm(jnp.concatenate([ref[count:] for ref in got], axis=0), up_ref[...], ROWS)
    parted(core_ref, out[:WIDE], out[WIDE:], out_ref, out_o_ref)


def run_early(core, normed, up, got):
    model = normed.shape[1]
    return pl.pallas_call(
        early_kernel,
        in_specs=[pl.BlockSpec(memory_space=pltpu.SMEM)] + [pl.BlockSpec(memory_space=pltpu.VMEM)] * 6,
        out_specs=[pl.BlockSpec(memory_space=pltpu.VMEM)] * 4,
        out_shape=[
            shape(2 * WIDE, model // 2), shape(2 * WIDE, model // 2, bf16), shape(WIDE, model), shape(WIDE, model, bf16),
        ],
        compiler_params=pltpu.CompilerParams(vmem_limit_bytes=24 * 1024 * 1024),
        cost_estimate=pl.CostEstimate(flops=1, bytes_accessed=1, transcendentals=0),
        name="early_products",
    )(core, normed, up, *got)


def late_kernel(core_ref, normed_ref, *refs):
    got, (late_ref, late_o_ref) = refs[:QUARTERS], refs[QUARTERS:]
    late = mm(jnp.concatenate([ref[...] for ref in got], axis=0), normed_ref[...], ROWS)
    half = late_ref.shape[1]
    parted(core_ref, late[:, :half], late[:, half:], late_ref, late_o_ref)


def run_late(core, normed, got):
    model = normed.shape[1]
    return pl.pallas_call(
        late_kernel,
        in_specs=[pl.BlockSpec(memory_space=pltpu.SMEM)] + [pl.BlockSpec(memory_space=pltpu.VMEM)] * 5,
        out_specs=[pl.BlockSpec(memory_space=pltpu.VMEM)] * 2,
        out_shape=[shape(LATE, model // 2), shape(LATE, model // 2, bf16)],
        compiler_params=pltpu.CompilerParams(vmem_limit_bytes=24 * 1024 * 1024),
        cost_estimate=pl.CostEstimate(flops=1, bytes_accessed=1, transcendentals=0),
        name="late_products",
    )(core, normed, *got)


def finish_kernel(side_ref, base_ref, first, first_got, second, second_got, out_ref, rows_s, sems):
    half = first.shape[0] // 2
    body, wide_cols = half - NSTATE, 2 * WIDE
    sizes = [wide_cols] * QUARTERS + [rows_s.shape[0] - INNER]
    moves = [
        pltpu.make_async_copy(
            rows_s.at[pl.ds(at * wide_cols, size)], out_ref.at[pl.ds(INNER + at * wide_cols, size)], sems.at[at]
        )
        for at, size in enumerate(sizes)
    ]
    for place in range(QUARTERS):
        x, y = place // 2, place % 2
        top = slice(y * half, (y + 1) * half)
        start = place * wide_cols
        rows_s[start : start + half] = jnp.where(side_ref[0] == x, first[top], first_got[top]).astype(f32)
        low = slice(x * half, (x + 1) * half)
        value = jnp.where(side_ref[1] == y, second[low], second_got[low]).astype(f32)
        rows_s[start + half : start + wide_cols] = value[:body]
        keep = min(NSTATE, max(0, rows_s.shape[0] - INNER - place * NSTATE))
        if keep:
            rows_s[INNER + place * NSTATE : INNER + place * NSTATE + keep] = value[body : body + keep]
        moves[place].start()
    moves[QUARTERS].start()
    for move in moves:
        move.wait()


def run_finish(sides, base, first, first_got, second, second_got):
    late_rows = base.shape[0] - INNER
    return pl.pallas_call(
        finish_kernel,
        in_specs=[pl.BlockSpec(memory_space=pltpu.SMEM), pl.BlockSpec(memory_space=pl.ANY)]
        + [pl.BlockSpec(memory_space=pltpu.VMEM)] * 4,
        out_specs=pl.BlockSpec(memory_space=pl.ANY),
        out_shape=jax.ShapeDtypeStruct(base.shape, f32),
        scratch_shapes=[pltpu.VMEM((late_rows, base.shape[1]), f32), pltpu.SemaphoreType.DMA((QUARTERS + 1,))],
        input_output_aliases={1: 0},
        compiler_params=pltpu.CompilerParams(vmem_limit_bytes=24 * 1024 * 1024),
        cost_estimate=pl.CostEstimate(flops=1, bytes_accessed=8_000_000, transcendentals=0),
        name="late_rows",
    )(sides, base, first, first_got, second, second_got)


def make_shards(mesh):
    reps = mesh.shape["rep"]
    bits = reps.bit_length() - 1
    assert reps == 1 << bits and bits >= 2 and mesh.shape["shard"] == 2
    up_order, down_order = tuple(range(2, bits)), tuple(reversed(range(2, bits)))
    far = len(up_order)

    def swap(value):
        return lax.ppermute(value, "shard", [(0, 1), (1, 0)])

    def across(value, flip):
        return lax.ppermute(value, "rep", [(place, place ^ flip) for place in range(reps)])

    def side_of(bit):
        return (lax.axis_index("rep") >> bit) & 1

    def quarter_of(flip):
        place = lax.axis_index("rep") ^ flip
        return (place & 1) * 2 + ((place >> 1) & 1)

    def joined(side, mine, theirs, axis):
        return jnp.where(
            side == 0, jnp.concatenate([mine, theirs], axis=axis), jnp.concatenate([theirs, mine], axis=axis)
        )

    def part(value, bit, flip):
        half = value.shape[0] // 2
        return lax.dynamic_slice_in_dim(value, (side_of(bit) ^ flip) * half, half)

    def terms(smalls):
        high = lax.reduce_precision(smalls, 8, 7)
        return jnp.concatenate([high.astype(bf16), (smalls - high).astype(bf16)], axis=0)

    def exchange(value, bit, smalls):
        if smalls is None:
            return across(value, 1 << bit), None
        rows, count = value.shape[0], smalls.shape[0]
        got = across(jnp.concatenate([value, terms(smalls)], axis=0), 1 << bit)
        added = got[rows:].astype(f32)
        return got[:rows], smalls + added[:count] + added[count:]

    def scatter(value, bit, smalls=None):
        got, smalls = exchange(part(value, bit, 1).astype(bf16), bit, smalls)
        return part(value, bit, 0) + got.astype(f32), smalls

    def gather(value, bit, smalls=None):
        got, smalls = exchange(value, bit, smalls)
        return joined(side_of(bit), value, got, 0), smalls

    def pair_step(pieces, at, smalls=None, carrier=1):
        beside = [None, None]
        beside[carrier] = smalls
        moved = []
        for which, value in enumerate(pieces):
            order = (up_order, down_order)[which]
            if at < far:
                moved.append(scatter(value, order[at], beside[which]))
            else:
                value = value.astype(bf16) if at == far else value
                late_at = at - 2 * far
                bit = order[2 * far - 1 - at] if late_at < 0 else (1 - late_at, late_at)[which]
                moved.append(gather(value, bit, beside[which]))
        return tuple(value for value, _ in moved), moved[carrier][1]

    steps = 2 * far + 2

    def turned(value):
        size = value.shape[0] // QUARTERS
        return [value[at * size : (at + 1) * size] for at in (0, 2, 1, 3)]

    def shards(
        tokens, lengths, norm_gain, in_weight, conv_weight, conv_bias, step_bias, decay_log, skip_gain,
        gate_gain, out_weight, cotangent,
    ):
        core = lax.axis_index("shard")
        rows, model = tokens.shape
        half_model, half_inner = model // 2, INNER // 2
        half_conv, half_heads = CONVDIM // 2, HEADS // 2

        def mine(value, size):
            return lax.dynamic_slice_in_dim(value, core * size, size, axis=1)

        def theirs(value, size):
            return lax.dynamic_slice_in_dim(value, (1 - core) * size, size, axis=1)

        known = run_pack(lengths, tokens, cotangent)
        upstream = known[rows:]
        known = [known, *(across(known, flip) for flip in (1, 2, 3))]

        def line(value):
            return jnp.pad(value, (0, half_conv - value.shape[0]))[None]

        small = jnp.concatenate(
            [
                conv_weight.T, conv_bias[None], line(gate_gain),
                line(jnp.concatenate([norm_gain, step_bias, decay_log, skip_gain])),
                jnp.zeros((1, half_conv), bf16),
            ],
            axis=0,
        )
        small_o = swap(small)
        in_other = swap(in_weight)
        out_other = swap(out_weight)
        small, small_o = small.astype(f32), small_o.astype(f32)
        low_half, high_half = jnp.where(core == 0, small, small_o), jnp.where(core == 0, small_o, small)
        both = jnp.concatenate([low_half, high_half], axis=1)

        def pick(row, start, size):
            return jnp.concatenate([low_half[row, start : start + size], high_half[row, start : start + size]])

        norm_scale = pick(6, 0, half_model)
        head_lines = [pick(6, half_model + at * half_heads, half_heads) for at in range(3)]
        gate_line = pick(5, 0, half_inner)[None]
        par = jnp.concatenate(
            [
                both[:5],
                jnp.pad(gate_line, ((0, 0), (0, CONVDIM - INNER))),
                jnp.pad(jnp.repeat(head_lines[2], HEADDIM)[None], ((0, 0), (0, CONVDIM - INNER))),
                jnp.zeros((1, CONVDIM), f32),
            ],
            axis=0,
        )
        head = jnp.pad(jnp.stack(head_lines[:2]), ((0, 6), (0, LANES - HEADS)))

        inputs = tokens.astype(f32)
        scale, normed = normalized(inputs, norm_scale)
        normed_m, normed_o = mine(normed, half_model), theirs(normed, half_model)

        gated_grad = joined(core, mm(upstream, out_weight, LANE), mm(upstream, out_other, LANE), 1)
        projected = mm(normed_m, in_weight) + mm(normed_o, in_other)
        raw = jnp.pad(projected[:, STEP_COL:], ((0, 0), (0, LANES - HEADS)))
        gated, dgate, leaving, dheads, heads, conv, convbc, gain_g = run_forward(
            lengths, raw, head, projected, gated_grad, par, gate_line
        )

        def quarters(value):
            return [lax.dynamic_index_in_dim(value, quarter_of(flip), 0, keepdims=False) for flip in range(QUARTERS)]

        early_sent = quarters(leaving)
        early_got = [early_sent[0], *(across(early_sent[flip], flip) for flip in (1, 2, 3))]
        dx, dr, late, total = run_backward(
            lengths, raw, head, projected, conv, convbc, dheads, heads, par, gain_g
        )

        late_sent = quarters(late)
        late_sent, known, dx, dr, dgate, gated = lax.optimization_barrier((late_sent, known, dx, dr, dgate, gated))
        place = core.astype(jnp.int32)[None]
        known_normed, known_up = run_known(norm_scale[None], known)
        gated_m, gated_o = mine(gated, half_inner), theirs(gated, half_inner)
        branch = mm(gated_m, out_weight) + mm(gated_o, out_other)
        live = (jnp.arange(rows, dtype=jnp.int32) < jnp.sum(lengths))[:, None]
        output = (inputs + jnp.where(live, branch, 0.0)).astype(bf16)
        proj_grad = jnp.concatenate([dgate, dx, dr[:, : CONVDIM - INNER + HEADS]], axis=1)
        normed_grad = joined(core, mm(proj_grad, in_weight, LANE), mm(proj_grad, in_other, LANE), 1)
        g = normed_grad * norm_scale
        input_grad = (
            cotangent.astype(f32)
            + scale * g
            - inputs * (scale * scale * scale * jnp.mean(g * inputs, axis=-1, keepdims=True))
        )
        gain_grad = jnp.sum(normed_grad * inputs * scale, axis=0)

        total = lax.dynamic_update_slice(total, gain_grad[None], (6, 0))
        early_got, output, input_grad, total = lax.optimization_barrier((early_got, output, input_grad, total))
        late_got = [late_sent[0], *(across(late_sent[flip], flip) for flip in (1, 2, 3))]
        gate_mine, gate_theirs, out_mine, out_theirs = run_early(place, known_normed, known_up, early_got)
        early = (out_mine + swap(out_theirs).astype(f32), gate_mine + swap(gate_theirs).astype(f32))
        early, _ = pair_step(early, 0)
        early, _ = pair_step(early, 1)
        early, late_got, total = lax.optimization_barrier((early, late_got, total))
        smalls = (total + swap(total)).reshape(-1, half_model)
        early, _ = pair_step(early, 2)
        late_mine, late_theirs = run_late(place, known_normed, late_got)
        late_theirs = swap(late_theirs)
        early, late_mine, late_theirs = lax.optimization_barrier((early, late_mine, late_theirs))
        early, _ = pair_step(early, 3)
        late_grad = late_mine + late_theirs.astype(f32)
        early, late_grad = lax.optimization_barrier((early, late_grad))
        half_late = LATE // 2
        late_parts = (late_grad[:half_late], late_grad[half_late:])
        last = 2 * far + 1
        last = 2 * far + 1
        for at in range(4, steps):
            early, smalls = pair_step(early, at, smalls) if at == last - 1 else (pair_step(early, at)[0], smalls)
            for late_at in {last - 1: range(far), last: range(far, 2 * far)}.get(at, ()):
                late_parts, added = pair_step(late_parts, late_at, smalls if late_at >= far else None)
                smalls = smalls if added is None else added
            if at >= last:
                early, late_parts = lax.optimization_barrier((early, late_parts))
        late_parts, smalls = pair_step(late_parts, steps - 2, smalls, 0)
        out_grad = early[0].astype(f32)
        late_parts, out_grad = lax.optimization_barrier((late_parts, out_grad))
        in_grad = jnp.concatenate(
            [*turned(early[1]), jnp.zeros((STEP_COL + HEADS - INNER, half_model), bf16)], axis=0
        ).astype(f32)
        total = smalls.reshape(total.shape)

        def own(row, start, size):
            return lax.dynamic_slice_in_dim(total[row], start + core * size, size)

        small_grads = (
            own(6, 0, half_model),
            lax.dynamic_slice_in_dim(total[:4], core * half_conv, half_conv, axis=1).T,
            own(4, 0, half_conv),
            own(6, HEAD_SUMS, half_heads),
            own(6, HEAD_SUMS + LANES, half_heads),
            own(6, HEAD_SUMS + 2 * LANES, half_heads),
            own(5, 0, half_inner),
        )
        in_grad, small_grads = lax.optimization_barrier((in_grad, small_grads))
        sides = jnp.stack([side_of(0), side_of(1)]).astype(jnp.int32)
        in_grad = run_finish(
            sides, in_grad, late_parts[0], across(late_parts[0], 1), late_parts[1], across(late_parts[1], 2)
        ).T
        norm_grad, conv_grad, bias_grad, step_grad, decay_grad, skip_grad, gate_grad = small_grads

        return (
            output, input_grad, norm_grad, in_grad, conv_grad, bias_grad, step_grad, decay_grad, skip_grad,
            gate_grad, out_grad,
        )

    return shards


def solution(mesh):
    split = P(("rep", "shard"), None)
    vector, matrix = P("shard"), P("shard", None)
    in_specs = (
        split, split, vector, matrix, matrix, vector, vector, vector, vector, vector, matrix, split,
    )
    out_specs = (
        split, split, vector, matrix, matrix, vector, vector, vector, vector, vector, matrix,
    )
    return jax.shard_map(make_shards(mesh), mesh=mesh, in_specs=in_specs, out_specs=out_specs, check_vma=False)
```
